32 devices in a mesh: groups: 2 (over y), ctx: 4 (over z), head: 2 (over x), sub: 2 (over core).
Axes of the slice: x: 2, y: 2, z: 4, core: 2. Of those that a mesh axis runs over, the one named last changes fastest.
Arguments:
- queries: bfloat16 [4096, 40, 128], P(('groups', 'ctx', 'sub'), 'head'), parts along dimension 0, may hold values from -35 to 35
- key_rows: bfloat16 [4096, 40, 128], P(('groups', 'ctx', 'sub'), 'head'), parts along dimension 0, may hold values from -4.5 to 4.5
- value_rows: bfloat16 [4096, 40, 128], P(('groups', 'ctx', 'sub'), 'head'), parts along dimension 0, may hold values from -16 to 16
- critical: int32 [64, 40, 16], P(('groups', 'ctx', 'sub'), 'head'), parts along dimension 0, may hold values from 0 to 31, as said below
- branch_weight: bfloat16 [128, 128], replicated, may hold values from -0.5 to 0.5
Outputs:
- attended: bfloat16 [4096, 40, 128], P(('groups', 'ctx', 'sub'), 'head'), parts along dimension 0
The draws below stay inside these ranges and needn't reach their ends.
There are 2 independent parts, one for each index of `groups`. The reference program is written for one: setup_inputs(seed, part) draws one part's arguments, and reference() takes and returns one part's arrays. A program takes and returns all parts, laid end to end along the dimension named above; an argument that names none is the same for every part. Nothing has to cross between parts.
Inputs may be any that keep to these rules, and one draw needn't show every extreme that they name: Each list critical[b, h, :] names 16 different key blocks. Its first entry is b itself, the next 3 are the following blocks of b's segment of 256 consecutive tokens, cyclically within the segment; the other 12 lie in other segments. Over all lists of one segment's query blocks and one group of 20 consecutive heads, at most 58 different (block, head) pairs lie in any one other segment, and exactly 58 in some.
All inputs are finite; a program needn't handle non-finite values.
Results may differ from the reference program's by a relative error of at most 0.004.
Values may be sent and summed in bfloat16 or wider, within the bound.
A program may use at most 128 MiB of HBM per device.

```python
import jax
import jax.numpy as jnp
from jax import lax

ATTENTION_HEADS = 40
HD = 128
ROWS = 256
TOPK = 16
LOCAL = 4
POOL = 20
SHARDS = 8
H_DEV = 20
LATENT_TOKENS = 2048


def key_table(key):
    first = jax.random.fold_in(jax.random.fold_in(key, 101), 0)
    table = jnp.clip(jax.random.normal(first, (LATENT_TOKENS, ATTENTION_HEADS, HD), jnp.float32), -4.5, 4.5)
    return table


def key_drift(key):
    slope_key = jax.random.fold_in(key, 404)
    slopes = 0.8 + 0.3 * jnp.clip(jax.random.normal(slope_key, (ATTENTION_HEADS, HD), jnp.float32), -2.5, 2.5)
    progress = -1.5 + 3.0 * jnp.arange(LATENT_TOKENS).astype(jnp.float32) / (LATENT_TOKENS - 1)
    return progress[:, None, None] * slopes[None, :, :]


def draw_key_rows(key, part):
    drifted = jnp.clip(key_table(key) + key_drift(key), -4.5, 4.5)
    return drifted.astype(jnp.bfloat16)


def draw_queries(key, part):
    noise_key = jax.random.fold_in(key, 202)
    base = jnp.clip(jax.random.normal(noise_key, (LATENT_TOKENS, ATTENTION_HEADS, HD), jnp.float32), -4.5, 4.5)
    return base.astype(jnp.bfloat16)


def draw_value_rows(key, part):
    first, second, third_fraction = jax.random.split(jax.random.fold_in(key, 303), 3)
    random_noise = jnp.clip(jax.random.normal(first, (LATENT_TOKENS, ATTENTION_HEADS, HD), jnp.float32), -4.5, 4.5)
    channel_index = 0.6 * jnp.clip(jax.random.normal(second, (ATTENTION_HEADS, HD), jnp.float32), -2.5, 2.5)
    linear_ramp = 1.0 + 2.0 * jnp.arange(LATENT_TOKENS).astype(jnp.float32) / (LATENT_TOKENS - 1)
    spike_pattern = jnp.exp(jax.random.uniform(third_fraction, (LATENT_TOKENS // 64, ATTENTION_HEADS), jnp.float32, jnp.log(0.4), jnp.log(2.5)))
    spike_row_list = jnp.repeat(spike_pattern, 64, axis=0)
    output_values = random_noise + channel_index[None, :, :] * (linear_ramp[:, None] * spike_row_list)[:, :, None]
    return output_values.astype(jnp.bfloat16)


def draw_critical(key, part):
    key_perm, key_rot, key_pick = jax.random.split(key, 3)
    group_count = ATTENTION_HEADS // H_DEV
    block_count = ROWS // 64
    other_count = SHARDS - 1
    perms = jax.vmap(lambda one_key: jax.random.permutation(one_key, other_count))(jax.random.split(key_perm, SHARDS * group_count))
    perms = perms.reshape(SHARDS, group_count, other_count)
    rotate = jax.random.randint(key_rot, (SHARDS, group_count), 0, block_count)
    order = jnp.arange(H_DEV * POOL)
    offset = 1 + perms[:, :, order % other_count]
    owner_shard = (jnp.arange(SHARDS)[:, None, None] + offset) % SHARDS
    same_owner = owner_shard[:, :, :, None] == owner_shard[:, :, None, :]
    earlier = order[None, :] < order[:, None]
    rank = jnp.sum(jnp.logical_and(same_owner, earlier[None, None]).astype(jnp.int32), axis=-1)
    block_local = (rank + rotate[:, :, None]) % block_count
    pool_ids = (owner_shard * block_count + block_local).reshape(SHARDS, ATTENTION_HEADS, POOL)
    picks = jax.vmap(lambda one_key: jax.random.permutation(one_key, POOL))(jax.random.split(key_pick, SHARDS * ATTENTION_HEADS))
    picks = picks.reshape(SHARDS, ATTENTION_HEADS, POOL)
    kept = (jnp.arange(block_count)[:, None] * 8 + 8 + jnp.arange(TOPK - LOCAL)[None, :]) % POOL
    chosen = picks[:, :, kept].reshape(SHARDS, ATTENTION_HEADS, block_count * (TOPK - LOCAL))
    remote = jnp.take_along_axis(pool_ids, chosen, axis=2).reshape(SHARDS, ATTENTION_HEADS, block_count, TOPK - LOCAL)
    remote = remote.transpose(0, 2, 1, 3)
    nearby = (jnp.arange(block_count)[:, None] + jnp.arange(LOCAL)[None, :]) % block_count
    nearby = jnp.arange(SHARDS)[:, None, None] * block_count + nearby[None, :, :]
    nearby = jnp.broadcast_to(nearby[:, :, None, :], (SHARDS, block_count, ATTENTION_HEADS, LOCAL))
    lists = jnp.concatenate([nearby, remote], axis=-1).reshape(SHARDS * block_count, ATTENTION_HEADS, TOPK)
    return lists.astype(jnp.int32)


def centred(rng, shape, deviation, most, dtype=jnp.bfloat16):
    result = deviation * jax.random.normal(rng, shape, jnp.float32)
    return jnp.clip(result, min=-most, max=most).astype(dtype)


def setup_inputs(seed: int = 0, part: int = 0) -> dict:
    splits = jax.random.split(jax.random.key(seed), 6)
    part_splits = jax.random.split(jax.random.fold_in(splits[5], part), 6)
    return {
        "queries": draw_queries(jax.random.fold_in(jax.random.fold_in(splits[5], part), 71), part),
        "key_rows": draw_key_rows(jax.random.fold_in(jax.random.fold_in(splits[5], part), 71), part),
        "value_rows": draw_value_rows(jax.random.fold_in(jax.random.fold_in(splits[5], part), 71), part),
        "critical": draw_critical(jax.random.fold_in(jax.random.fold_in(splits[5], part), 71), part),
        "branch_weight": centred(splits[4], (HD, HD), HD ** -0.5, 0.5),
    }


def feature(values_in):
    return jax.nn.elu(values_in) + 1.0


def reference(queries, key_rows, value_rows, critical, branch_weight):
    seq_count, head_count, head_width = queries.shape
    block_count = seq_count // 64
    softmax_scale = head_width ** -0.5
    key_feature = feature(key_rows.astype(jnp.float32)).astype(jnp.bfloat16)
    query_feature = feature(queries.astype(jnp.float32)).astype(jnp.bfloat16)
    kv_state = jnp.einsum("thd,the->hde", key_feature.astype(jnp.float32), value_rows.astype(jnp.float32), precision=lax.Precision.HIGHEST)
    key_total = jnp.sum(key_feature.astype(jnp.float32), axis=0)

    def one_head(inputs):
        query_head, qfeat_head, key_head, value_head, kfeat_head, list_head, head_state_matrix, head_key_total = inputs
        nearby_key_rows = key_head.reshape(block_count, 64, head_width)[list_head].reshape(block_count, -1, head_width)
        nearby_value_rows = value_head.reshape(block_count, 64, head_width)[list_head].reshape(block_count, -1, head_width)
        nearby_key_features = kfeat_head.reshape(block_count, 64, head_width)[list_head].reshape(block_count, -1, head_width)
        query_block_rows = query_head.reshape(block_count, 64, head_width).astype(jnp.float32)
        query_feature_block = qfeat_head.reshape(block_count, 64, head_width).astype(jnp.float32)
        score_matrix = jnp.einsum("twa,tpa->twp", query_block_rows, nearby_key_rows.astype(jnp.float32)) * softmax_scale
        top_score = jnp.max(score_matrix, axis=-1, keepdims=True)
        expo_scores = jnp.exp(score_matrix - top_score)
        softmax_weights = (expo_scores / jnp.sum(expo_scores, axis=-1, keepdims=True)).astype(jnp.bfloat16)
        sparse_output = jnp.einsum("mgw,mwa->mga", softmax_weights.astype(jnp.float32), nearby_value_rows.astype(jnp.float32))
        nearby_score_matrix = jnp.einsum("twa,tpa->twp", query_feature_block, nearby_key_features.astype(jnp.float32))
        nearby_weight_matrix = nearby_score_matrix.astype(jnp.bfloat16)
        nearby_numerator = jnp.einsum("mgw,mwa->mga", nearby_weight_matrix.astype(jnp.float32), nearby_value_rows.astype(jnp.float32))
        nearby_denominator = jnp.sum(nearby_score_matrix, axis=-1)
        linear_numerator = jnp.einsum("gfh,ht->gft", query_feature_block, head_state_matrix, precision=lax.Precision.HIGHEST) - nearby_numerator
        linear_denominator = jnp.einsum("tay,y->ta", query_feature_block, head_key_total, precision=lax.Precision.HIGHEST) - nearby_denominator
        linear_part = (linear_numerator / linear_denominator[..., None]).astype(jnp.bfloat16)
        projected = jnp.dot(linear_part.reshape(-1, head_width), branch_weight, preferred_element_type=jnp.float32)
        mixed_rows = sparse_output.reshape(-1, head_width) + projected
        return mixed_rows.astype(jnp.bfloat16)

    attended = lax.map(one_head, (queries.transpose(1, 0, 2), query_feature.transpose(1, 0, 2), key_rows.transpose(1, 0, 2), value_rows.transpose(1, 0, 2), key_feature.transpose(1, 0, 2), critical.transpose(1, 0, 2), kv_state, key_total))
    return attended.transpose(1, 0, 2)
```

```python
import functools
import math

import jax
import jax.numpy as jnp
from jax import lax
from jax.experimental import pallas as pl
from jax.experimental.pallas import tpu as pltpu
from jax.sharding import PartitionSpec as P


def as_sent(array):

    def short(part):
        return part.astype(jnp.bfloat16) if part.dtype == jnp.float32 else part

    return jax.tree.map(short, array)


def feature(values_in):
    return jax.nn.elu(values_in) + 1.0


def attend_pair(inputs, pool_keys, pool_values, branch_weight, softmax_scale):
    query_block_rows, query_feature, pool_index, pair_state, pair_total = inputs
    block_count = query_block_rows.shape[0]
    head_width = query_block_rows.shape[-1]
    nearby_key_rows = jnp.take(pool_keys, pool_index.reshape(-1), axis=0).reshape(
        block_count, 2, -1, head_width
    )
    nearby_value_rows = jnp.take(pool_values, pool_index.reshape(-1), axis=0).reshape(
        block_count, 2, -1, head_width
    )
    score_matrix = (
        jnp.einsum(
            "bhqd,bhkd->bhqk", query_block_rows, nearby_key_rows, preferred_element_type=jnp.float32
        )
        * softmax_scale
    )
    top_score = jnp.max(score_matrix, axis=-1, keepdims=True)
    expo_scores = jnp.exp(score_matrix - top_score)
    softmax_weights = (expo_scores / jnp.sum(expo_scores, axis=-1, keepdims=True)).astype(
        jnp.bfloat16
    )
    sparse_output = jnp.einsum(
        "bhqk,bhkd->bhqd", softmax_weights, nearby_value_rows, preferred_element_type=jnp.float32
    )
    nearby_key_features = feature(nearby_key_rows.astype(jnp.float32)).astype(jnp.bfloat16)
    nearby_score_matrix = jnp.einsum(
        "bhqd,bhkd->bhqk", query_feature, nearby_key_features, preferred_element_type=jnp.float32
    )
    nearby_weight_matrix = nearby_score_matrix.astype(jnp.bfloat16)
    nearby_numerator = jnp.einsum(
        "bhqk,bhkd->bhqd",
        nearby_weight_matrix,
        nearby_value_rows,
        preferred_element_type=jnp.float32,
    )
    nearby_denominator = jnp.sum(nearby_score_matrix, axis=-1)
    feature_wide = query_feature.astype(jnp.float32)
    linear_numerator = (
        jnp.einsum("bhqd,hde->bhqe", feature_wide, pair_state, precision=lax.Precision.HIGHEST)
        - nearby_numerator
    )
    linear_denominator = (
        jnp.einsum("bhqd,hd->bhq", feature_wide, pair_total, precision=lax.Precision.HIGHEST)
        - nearby_denominator
    )
    linear_part = (linear_numerator / linear_denominator[..., None]).astype(jnp.bfloat16)
    projected = jnp.einsum(
        "bhqd,de->bhqe", linear_part, branch_weight, preferred_element_type=jnp.float32
    )
    return (sparse_output + projected).astype(jnp.bfloat16)


def on_device(queries, key_rows, value_rows, critical, branch_weight):
    row_count, head_count, head_width = queries.shape
    list_length = critical.shape[-1]
    block_count = row_count // 64
    shard_count = lax.axis_size(("ctx", "sub"))
    myself = lax.axis_index(("ctx", "sub"))
    local_count = min(block_count, 8)
    pool_size = 24 - local_count
    capacity = (head_count * pool_size + shard_count - 2) // (shard_count - 1)
    softmax_scale = head_width ** (-0.5)
    key_feature = feature(key_rows.astype(jnp.float32)).astype(jnp.bfloat16)
    query_feature = feature(queries.astype(jnp.float32)).astype(jnp.bfloat16)
    kv_state = jnp.einsum(
        "thd,the->hde", key_feature, value_rows, preferred_element_type=jnp.float32
    )
    key_total = jnp.sum(key_feature, axis=0, dtype=jnp.float32)
    kv_state, key_total = lax.psum((kv_state, key_total), ("ctx", "sub"))
    pair_slots = block_count * head_count
    block_owner = critical // block_count
    block_local = critical % block_count
    slot_code = block_local * head_count + jnp.arange(head_count, dtype=jnp.int32)[None, :, None]
    every_block = jnp.arange(shard_count * block_count, dtype=jnp.int32)
    hit_counts = jnp.sum((critical[..., None] == every_block).astype(jnp.int32), axis=(0, 2))
    wanted = (
        hit_counts.reshape(head_count, shard_count, block_count)
        .transpose(1, 2, 0)
        .reshape(shard_count, pair_slots)
        > 0
    )
    wanted = jnp.logical_and(wanted, jnp.arange(shard_count, dtype=jnp.int32)[:, None] != myself)
    slot_place = jnp.cumsum(wanted.astype(jnp.int32), axis=1) - 1
    slot_match = jnp.logical_and(
        wanted[:, :, None],
        slot_place[:, :, None] == jnp.arange(capacity, dtype=jnp.int32)[None, None, :],
    )
    code_values = jnp.sum(
        jnp.where(slot_match, jnp.arange(pair_slots, dtype=jnp.int32)[None, :, None], 0), axis=1
    )
    asked_codes = jnp.where(jnp.any(slot_match, axis=1), code_values, -1)
    local_keys = (
        key_rows.reshape(block_count, 64, head_count, head_width)
        .transpose(0, 2, 1, 3)
        .reshape(pair_slots, 64, head_width)
    )
    local_values = (
        value_rows.reshape(block_count, 64, head_count, head_width)
        .transpose(0, 2, 1, 3)
        .reshape(pair_slots, 64, head_width)
    )
    picked = jnp.clip(
        lax.all_to_all(asked_codes, ("ctx", "sub"), split_axis=0, concat_axis=0, tiled=True),
        0,
        pair_slots - 1,
    )
    far_keys, far_values = lax.all_to_all(
        as_sent((jnp.take(local_keys, picked, axis=0), jnp.take(local_values, picked, axis=0))),
        ("ctx", "sub"),
        split_axis=0,
        concat_axis=0,
        tiled=True,
    )
    pool_keys = jnp.concatenate(
        [local_keys, far_keys.reshape(shard_count * capacity, 64, head_width)], axis=0
    )
    pool_values = jnp.concatenate(
        [local_values, far_values.reshape(shard_count * capacity, 64, head_width)], axis=0
    )
    flat_index = block_owner * pair_slots + slot_code
    slot_table = jnp.where(wanted, slot_place, 0).reshape(-1)
    table_range = jnp.arange(shard_count * pair_slots, dtype=jnp.int32)
    slot_found = jnp.sum(jnp.where(flat_index[..., None] == table_range, slot_table, 0), axis=-1)
    pool_index = jnp.where(
        block_owner == myself, slot_code, pair_slots + block_owner * capacity + slot_found
    )
    pair_count = head_count // 2
    query_pairs = queries.reshape(block_count, 64, pair_count, 2, head_width).transpose(
        2, 0, 3, 1, 4
    )
    feature_pairs = query_feature.reshape(block_count, 64, pair_count, 2, head_width).transpose(
        2, 0, 3, 1, 4
    )
    index_pairs = pool_index.reshape(block_count, pair_count, 2, list_length).transpose(1, 0, 2, 3)
    state_pairs = kv_state.reshape(pair_count, 2, head_width, head_width)
    total_pairs = key_total.reshape(pair_count, 2, head_width)
    attended = lax.map(
        lambda inputs: attend_pair(inputs, pool_keys, pool_values, branch_weight, softmax_scale),
        (query_pairs, feature_pairs, index_pairs, state_pairs, total_pairs),
    )
    return attended.transpose(1, 3, 0, 2, 4).reshape(row_count, head_count, head_width)


BLOCK = 64


def wide_feature(rows):
    wide = rows.astype(jnp.float32)
    return jnp.where(wide > 0, wide + 1.0, jnp.exp(jnp.minimum(wide, 0.0)))


def by_heads_kernel(dims, *refs):
    chips, heads, rows, width, listed = dims
    q_ref, k_ref, v_ref, lists_ref, weight_ref, out_ref = refs[:6]
    refs = refs[6:]
    q_bufs, refs = refs[:heads], refs[heads:]
    k_bufs, refs = refs[:heads], refs[heads:]
    v_bufs, refs = refs[:heads], refs[heads:]
    o_bufs, refs = refs[:heads], refs[heads:]
    (lists_in, lists, states, totals, state_sum, total_sum) = refs[:6]
    (send, recv, own, pair_send, pair_recv, out_send, out_recv, out_own) = refs[6:14]
    list_send, list_recv, list_own = refs[14:]
    group = lax.axis_index("groups")
    chip = lax.axis_index("ctx")
    column = lax.axis_index("head")
    core = lax.axis_index("sub")
    blocks = rows // BLOCK
    half = chips * blocks
    mate = (group, chip, column, 1 - core)

    def peer(step):
        other = lax.rem(chip + step, chips)
        return other, (group, other, column, core)

    barrier = pltpu.get_barrier_semaphore()
    for step in range(1, chips):
        pl.semaphore_signal(barrier, inc=1, device_id=peer(step)[1], device_id_type=pl.DeviceIdType.MESH)
    pl.semaphore_signal(barrier, inc=1, device_id=mate, device_id_type=pl.DeviceIdType.MESH)
    pl.semaphore_wait(barrier, chips)

    def remote(src, dst, send_sem, recv_sem, device):
        return pltpu.make_async_remote_copy(
            src_ref=src,
            dst_ref=dst,
            send_sem=send_sem,
            recv_sem=recv_sem,
            device_id=device,
            device_id_type=pl.DeviceIdType.MESH,
        )

    def near_rows(place):
        return pl.ds(core * half + place * blocks, blocks)

    def q_rows(place):
        return pl.ds(place * blocks, blocks)

    def landing(item, h, place):
        if item == 2:
            return q_bufs[h].at[q_rows(place)]
        return (k_bufs, v_bufs)[item][h].at[near_rows(place)]

    sources = (k_ref, v_ref, q_ref)

    def piece(item, h, step):
        other, device = peer(step)
        return remote(
            sources[item].at[other * heads + h],
            landing(item, h, chip),
            send.at[h, item, step],
            recv.at[h, item, step],
            device,
        )

    def arriving(item, h, step):
        sender = lax.rem(chip + chips - step, chips)
        return remote(
            sources[item].at[h],
            landing(item, h, sender),
            send.at[h, item, step],
            recv.at[h, item, step],
            peer(step)[1],
        )

    def own_piece(item, h):
        return pltpu.make_async_copy(
            sources[item].at[chip * heads + h], landing(item, h, chip), own.at[h, item]
        )

    def list_piece(step):
        other, device = peer(step)
        return remote(
            lists_ref.at[other], lists_in.at[chip], list_send.at[step], list_recv.at[step], device
        )

    def list_arriving(step):
        sender = lax.rem(chip + chips - step, chips)
        return remote(
            lists_ref.at[0], lists_in.at[sender], list_send.at[step], list_recv.at[step], peer(step)[1]
        )

    list_own_copy = pltpu.make_async_copy(lists_ref.at[chip], lists_in.at[chip], list_own.at[0])
    steps = list(range(1, chips))
    for step in steps:
        list_piece(step).start()
    list_own_copy.start()
    for h in range(heads):
        for item in range(3):
            own_piece(item, h).start()
            for step in steps:
                piece(item, h, step).start()
    for step in steps:
        list_arriving(step).wait_recv()
    list_own_copy.wait()
    to_scalars = pltpu.make_async_copy(lists_in, lists, list_own.at[1])
    to_scalars.start()
    to_scalars.wait()

    def pair_piece(item, h):
        mine = pl.ds(core * half, half)
        buf = (k_bufs, v_bufs)[item][h]
        return remote(
            buf.at[mine], buf.at[mine], pair_send.at[h, item], pair_recv.at[h, item], mate
        )

    def pair_arriving(item, h):
        other = pl.ds((1 - core) * half, half)
        buf = (k_bufs, v_bufs)[item][h]
        return remote(
            buf.at[other], buf.at[other], pair_send.at[h, item], pair_recv.at[h, item], mate
        )

    def out_piece(h, step):
        other, device = peer(step)
        return remote(
            o_bufs[h].at[q_rows(other)],
            out_ref.at[chip * heads + h],
            out_send.at[h, step],
            out_recv.at[h, step],
            device,
        )

    def out_arriving(h, step):
        sender = lax.rem(chip + chips - step, chips)
        return remote(
            o_bufs[h].at[q_rows(sender)],
            out_ref.at[sender * heads + h],
            out_send.at[h, step],
            out_recv.at[h, step],
            peer(step)[1],
        )

    def out_own_piece(h):
        return pltpu.make_async_copy(
            o_bufs[h].at[q_rows(chip)], out_ref.at[chip * heads + h], out_own.at[h]
        )

    exponent_scale = math.log2(math.e) / math.sqrt(width)
    for h in range(heads):
        for item in range(2):
            own_piece(item, h).wait()
            for step in steps:
                arriving(item, h, step).wait_recv()
            pair_piece(item, h).start()
        own_piece(2, h).wait()
        for step in steps:
            arriving(2, h, step).wait_recv()
        for item in range(2):
            pair_arriving(item, h).wait_recv()

        k_buf, v_buf, q_buf, o_buf = k_bufs[h], v_bufs[h], q_bufs[h], o_bufs[h]
        state_sum[...] = jnp.zeros_like(state_sum)
        total_sum[...] = jnp.zeros_like(total_sum)

        def one_state(j, carry):
            narrow = wide_feature(k_buf[j]).astype(jnp.bfloat16)
            state = lax.dot_general(
                narrow, v_buf[j], (((0,), (0,)), ((), ())), preferred_element_type=jnp.float32
            )
            total = jnp.sum(narrow.astype(jnp.float32).reshape(BLOCK // 8, 8, width), axis=0)
            states[j] = state
            totals[j] = total
            state_sum[...] += state
            total_sum[...] += total
            return carry

        lax.fori_loop(0, 2 * chips * blocks, one_state, 0, unroll=4)

        def one_block(b, carry):
            place = b // blocks
            base = lax.rem(b, blocks) * listed
            picks = [lists[place, h, base + i] for i in range(listed)]
            query = q_buf[b]
            near_keys = jnp.concatenate([k_buf[pick] for pick in picks], axis=0)
            near_values = jnp.concatenate([v_buf[pick] for pick in picks], axis=0)
            scores = lax.dot_general(
                query, near_keys, (((1,), (1,)), ((), ())), preferred_element_type=jnp.float32
            )
            top = jnp.max(scores, axis=-1, keepdims=True)
            expo = jnp.exp2((scores - top) * exponent_scale)
            mass = jnp.sum(expo, axis=-1, keepdims=True)
            sparse = jnp.dot(
                expo.astype(jnp.bfloat16), near_values, preferred_element_type=jnp.float32
            )
            state = states[picks[0]]
            total = totals[picks[0]]
            for pick in picks[1:]:
                state = state + states[pick]
                total = total + totals[pick]
            state = state_sum[...] - state
            total = jnp.sum(total_sum[...] - total, axis=0, keepdims=True)
            coarse = state.astype(jnp.bfloat16)
            fine = (state - coarse.astype(jnp.float32)).astype(jnp.bfloat16)
            narrow = wide_feature(query).astype(jnp.bfloat16)
            numerator = jnp.dot(narrow, coarse, preferred_element_type=jnp.float32) + jnp.dot(
                narrow, fine, preferred_element_type=jnp.float32
            )
            denominator = jnp.sum(narrow.astype(jnp.float32) * total, axis=-1, keepdims=True)
            linear = (numerator / denominator).astype(jnp.bfloat16)
            projected = jnp.dot(linear, weight_ref[...], preferred_element_type=jnp.float32)
            o_buf[b] = (sparse / mass + projected).astype(jnp.bfloat16)
            return carry

        lax.fori_loop(0, chips * blocks, one_block, 0, unroll=2)
        for step in steps:
            out_piece(h, step).start()
        out_own_piece(h).start()

    for h in range(heads):
        for item in range(3):
            for step in steps:
                piece(item, h, step).wait_send()
        for item in range(2):
            pair_piece(item, h).wait_send()
        out_own_piece(h).wait()
        for step in steps:
            out_piece(h, step).wait_send()
            out_arriving(h, step).wait_recv()
    for step in steps:
        list_piece(step).wait_send()


def head_major(array):
    rows, heads, width = array.shape
    return array.transpose(1, 0, 2).reshape(heads, rows // BLOCK, BLOCK, width)


def by_heads(queries, key_rows, value_rows, critical, branch_weight):
    rows, all_heads, width = queries.shape
    listed = critical.shape[-1]
    blocks = rows // BLOCK
    chips = lax.axis_size("ctx")
    heads = all_heads // chips
    shard = critical // blocks
    place = (shard % 2) * (chips * blocks) + (shard // 2) * blocks + critical % blocks
    lists = place.transpose(1, 0, 2).reshape(chips, heads, blocks * listed)
    lists = jnp.pad(lists, ((0, 0), (0, -heads % 8), (0, -(blocks * listed) % 128)))
    dims = (chips, heads, rows, width, listed)
    hbm = pl.BlockSpec(memory_space=pl.ANY)
    vmem = pl.BlockSpec(memory_space=pltpu.VMEM)
    near = pltpu.VMEM((2 * chips * blocks, BLOCK, width), jnp.bfloat16)
    mine = pltpu.VMEM((chips * blocks, BLOCK, width), jnp.bfloat16)
    sem = pltpu.SemaphoreType.DMA
    all_blocks = 2 * chips * blocks
    pairs = heads * chips * blocks
    out = pl.pallas_call(
        functools.partial(by_heads_kernel, dims),
        out_shape=jax.ShapeDtypeStruct((all_heads, blocks, BLOCK, width), jnp.bfloat16),
        in_specs=[hbm, hbm, hbm, hbm, vmem],
        out_specs=hbm,
        scratch_shapes=[mine] * heads
        + [near] * heads
        + [near] * heads
        + [mine] * heads
        + [
            pltpu.VMEM(lists.shape, jnp.int32),
            pltpu.SMEM(lists.shape, jnp.int32),
            pltpu.VMEM((all_blocks, width, width), jnp.float32),
            pltpu.VMEM((all_blocks, 8, width), jnp.float32),
            pltpu.VMEM((width, width), jnp.float32),
            pltpu.VMEM((8, width), jnp.float32),
            sem((heads, 3, chips)),
            sem((heads, 3, chips)),
            sem((heads, 3)),
            sem((heads, 2)),
            sem((heads, 2)),
            sem((heads, chips)),
            sem((heads, chips)),
            sem((heads,)),
            sem((chips,)),
            sem((chips,)),
            sem((2,)),
        ],
        compiler_params=pltpu.CompilerParams(
            collective_id=0, has_side_effects=True, vmem_limit_bytes=56 * 1024 * 1024
        ),
        cost_estimate=pl.CostEstimate(
            flops=pairs * 4 * BLOCK * BLOCK * listed * width,
            bytes_accessed=8 * all_heads * rows * width,
            transcendentals=pairs * BLOCK * BLOCK * listed,
        ),
    )(
        head_major(queries),
        head_major(key_rows),
        head_major(value_rows),
        lists,
        branch_weight,
    )
    return out.reshape(all_heads, rows, width).transpose(1, 0, 2)


def heads_fit(mesh, queries, critical):
    chips, cores = mesh.shape["ctx"], mesh.shape["sub"]
    shards = mesh.shape["groups"] * chips * cores
    rows = queries.shape[0] // shards
    heads = queries.shape[1] // mesh.shape["head"]
    if cores != 2 or heads % chips or chips < 2 or rows % BLOCK:
        return False
    width = queries.shape[2]
    tokens = chips * cores * rows
    held = heads // chips * tokens * width * 2 * 3
    states = tokens // BLOCK * (width + 8) * width * 4
    return held + states < 40 * 1024 * 1024


def solution(mesh):
    in_specs = (
        P(("groups", "ctx", "sub"), "head", None),
        P(("groups", "ctx", "sub"), "head", None),
        P(("groups", "ctx", "sub"), "head", None),
        P(("groups", "ctx", "sub"), "head", None),
        P(),
    )
    out_specs = P(("groups", "ctx", "sub"), "head", None)

    def run(queries, key_rows, value_rows, critical, branch_weight):
        body = by_heads if heads_fit(mesh, queries, critical) else on_device
        mapped = jax.shard_map(
            body, mesh=mesh, in_specs=in_specs, out_specs=out_specs, check_vma=False
        )
        return mapped(queries, key_rows, value_rows, critical, branch_weight)

    return run
```

```python
import functools
import math

import jax
import jax.numpy as jnp
from jax import lax
from jax.experimental import pallas as pl
from jax.experimental.pallas import tpu as pltpu
from jax.sharding import PartitionSpec as P


def as_sent(array):

    def short(part):
        return part.astype(jnp.bfloat16) if part.dtype == jnp.float32 else part

    return jax.tree.map(short, array)


def feature(values_in):
    return jax.nn.elu(values_in) + 1.0


def attend_pair(inputs, pool_keys, pool_values, branch_weight, softmax_scale):
    query_block_rows, query_feature, pool_index, pair_state, pair_total = inputs
    block_count = query_block_rows.shape[0]
    head_width = query_block_rows.shape[-1]
    nearby_key_rows = jnp.take(pool_keys, pool_index.reshape(-1), axis=0).reshape(
        block_count, 2, -1, head_width
    )
    nearby_value_rows = jnp.take(pool_values, pool_index.reshape(-1), axis=0).reshape(
        block_count, 2, -1, head_width
    )
    score_matrix = (
        jnp.einsum(
            "bhqd,bhkd->bhqk", query_block_rows, nearby_key_rows, preferred_element_type=jnp.float32
        )
        * softmax_scale
    )
    top_score = jnp.max(score_matrix, axis=-1, keepdims=True)
    expo_scores = jnp.exp(score_matrix - top_score)
    softmax_weights = (expo_scores / jnp.sum(expo_scores, axis=-1, keepdims=True)).astype(
        jnp.bfloat16
    )
    sparse_output = jnp.einsum(
        "bhqk,bhkd->bhqd", softmax_weights, nearby_value_rows, preferred_element_type=jnp.float32
    )
    nearby_key_features = feature(nearby_key_rows.astype(jnp.float32)).astype(jnp.bfloat16)
    nearby_score_matrix = jnp.einsum(
        "bhqd,bhkd->bhqk", query_feature, nearby_key_features, preferred_element_type=jnp.float32
    )
    nearby_weight_matrix = nearby_score_matrix.astype(jnp.bfloat16)
    nearby_numerator = jnp.einsum(
        "bhqk,bhkd->bhqd",
        nearby_weight_matrix,
        nearby_value_rows,
        preferred_element_type=jnp.float32,
    )
    nearby_denominator = jnp.sum(nearby_score_matrix, axis=-1)
    feature_wide = query_feature.astype(jnp.float32)
    linear_numerator = (
        jnp.einsum("bhqd,hde->bhqe", feature_wide, pair_state, precision=lax.Precision.HIGHEST)
        - nearby_numerator
    )
    linear_denominator = (
        jnp.einsum("bhqd,hd->bhq", feature_wide, pair_total, precision=lax.Precision.HIGHEST)
        - nearby_denominator
    )
    linear_part = (linear_numerator / linear_denominator[..., None]).astype(jnp.bfloat16)
    projected = jnp.einsum(
        "bhqd,de->bhqe", linear_part, branch_weight, preferred_element_type=jnp.float32
    )
    return (sparse_output + projected).astype(jnp.bfloat16)


def on_device(queries, key_rows, value_rows, critical, branch_weight):
    row_count, head_count, head_width = queries.shape
    list_length = critical.shape[-1]
    block_count = row_count // 64
    shard_count = lax.axis_size(("ctx", "sub"))
    myself = lax.axis_index(("ctx", "sub"))
    local_count = min(block_count, 8)
    pool_size = 24 - local_count
    capacity = (head_count * pool_size + shard_count - 2) // (shard_count - 1)
    softmax_scale = head_width ** (-0.5)
    key_feature = feature(key_rows.astype(jnp.float32)).astype(jnp.bfloat16)
    query_feature = feature(queries.astype(jnp.float32)).astype(jnp.bfloat16)
    kv_state = jnp.einsum(
        "thd,the->hde", key_feature, value_rows, preferred_element_type=jnp.float32
    )
    key_total = jnp.sum(key_feature, axis=0, dtype=jnp.float32)
    kv_state, key_total = lax.psum((kv_state, key_total), ("ctx", "sub"))
    pair_slots = block_count * head_count
    block_owner = critical // block_count
    block_local = critical % block_count
    slot_code = block_local * head_count + jnp.arange(head_count, dtype=jnp.int32)[None, :, None]
    every_block = jnp.arange(shard_count * block_count, dtype=jnp.int32)
    hit_counts = jnp.sum((critical[..., None] == every_block).astype(jnp.int32), axis=(0, 2))
    wanted = (
        hit_counts.reshape(head_count, shard_count, block_count)
        .transpose(1, 2, 0)
        .reshape(shard_count, pair_slots)
        > 0
    )
    wanted = jnp.logical_and(wanted, jnp.arange(shard_count, dtype=jnp.int32)[:, None] != myself)
    slot_place = jnp.cumsum(wanted.astype(jnp.int32), axis=1) - 1
    slot_match = jnp.logical_and(
        wanted[:, :, None],
        slot_place[:, :, None] == jnp.arange(capacity, dtype=jnp.int32)[None, None, :],
    )
    code_values = jnp.sum(
        jnp.where(slot_match, jnp.arange(pair_slots, dtype=jnp.int32)[None, :, None], 0), axis=1
    )
    asked_codes = jnp.where(jnp.any(slot_match, axis=1), code_values, -1)
    local_keys = (
        key_rows.reshape(block_count, 64, head_count, head_width)
        .transpose(0, 2, 1, 3)
        .reshape(pair_slots, 64, head_width)
    )
    local_values = (
        value_rows.reshape(block_count, 64, head_count, head_width)
        .transpose(0, 2, 1, 3)
        .reshape(pair_slots, 64, head_width)
    )
    picked = jnp.clip(
        lax.all_to_all(asked_codes, ("ctx", "sub"), split_axis=0, concat_axis=0, tiled=True),
        0,
        pair_slots - 1,
    )
    far_keys, far_values = lax.all_to_all(
        as_sent((jnp.take(local_keys, picked, axis=0), jnp.take(local_values, picked, axis=0))),
        ("ctx", "sub"),
        split_axis=0,
        concat_axis=0,
        tiled=True,
    )
    pool_keys = jnp.concatenate(
        [local_keys, far_keys.reshape(shard_count * capacity, 64, head_width)], axis=0
    )
    pool_values = jnp.concatenate(
        [local_values, far_values.reshape(shard_count * capacity, 64, head_width)], axis=0
    )
    flat_index = block_owner * pair_slots + slot_code
    slot_table = jnp.where(wanted, slot_place, 0).reshape(-1)
    table_range = jnp.arange(shard_count * pair_slots, dtype=jnp.int32)
    slot_found = jnp.sum(jnp.where(flat_index[..., None] == table_range, slot_table, 0), axis=-1)
    pool_index = jnp.where(
        block_owner == myself, slot_code, pair_slots + block_owner * capacity + slot_found
    )
    pair_count = head_count // 2
    query_pairs = queries.reshape(block_count, 64, pair_count, 2, head_width).transpose(
        2, 0, 3, 1, 4
    )
    feature_pairs = query_feature.reshape(block_count, 64, pair_count, 2, head_width).transpose(
        2, 0, 3, 1, 4
    )
    index_pairs = pool_index.reshape(block_count, pair_count, 2, list_length).transpose(1, 0, 2, 3)
    state_pairs = kv_state.reshape(pair_count, 2, head_width, head_width)
    total_pairs = key_total.reshape(pair_count, 2, head_width)
    attended = lax.map(
        lambda inputs: attend_pair(inputs, pool_keys, pool_values, branch_weight, softmax_scale),
        (query_pairs, feature_pairs, index_pairs, state_pairs, total_pairs),
    )
    return attended.transpose(1, 3, 0, 2, 4).reshape(row_count, head_count, head_width)


BLOCK = 64


def wide_feature(rows):
    wide = rows.astype(jnp.float32)
    return jnp.where(wide > 0, wide + 1.0, jnp.exp(jnp.minimum(wide, 0.0)))


def by_heads_kernel(dims, *refs):
    chips, heads, rows, width = dims
    q_ref, k_ref, v_ref, lists_ref, weight_ref, out_ref = refs[:6]
    refs = refs[6:]
    q_bufs, refs = refs[:heads], refs[heads:]
    k_bufs, refs = refs[:heads], refs[heads:]
    v_bufs, refs = refs[:heads], refs[heads:]
    o_bufs, refs = refs[:heads], refs[heads:]
    lists_in, members, features = refs[:3]
    (send, recv, own, pair_send, pair_recv, out_send, out_recv, out_own) = refs[3:11]
    list_send, list_recv, list_own = refs[11:]
    group = lax.axis_index("groups")
    chip = lax.axis_index("ctx")
    column = lax.axis_index("head")
    core = lax.axis_index("sub")
    blocks = rows // BLOCK
    half = chips * blocks
    mate = (group, chip, column, 1 - core)

    def peer(step):
        other = lax.rem(chip + step, chips)
        return other, (group, other, column, core)

    barrier = pltpu.get_barrier_semaphore()
    for step in range(1, chips):
        pl.semaphore_signal(barrier, inc=1, device_id=peer(step)[1], device_id_type=pl.DeviceIdType.MESH)
    pl.semaphore_signal(barrier, inc=1, device_id=mate, device_id_type=pl.DeviceIdType.MESH)
    pl.semaphore_wait(barrier, chips)

    def remote(src, dst, send_sem, recv_sem, device):
        return pltpu.make_async_remote_copy(
            src_ref=src,
            dst_ref=dst,
            send_sem=send_sem,
            recv_sem=recv_sem,
            device_id=device,
            device_id_type=pl.DeviceIdType.MESH,
        )

    def near_rows(place):
        return pl.ds(core * half + place * blocks, blocks)

    def q_rows(place):
        return pl.ds(place * blocks, blocks)

    def landing(item, h, place):
        if item == 2:
            return q_bufs[h].at[q_rows(place)]
        return (k_bufs, v_bufs)[item][h].at[near_rows(place)]

    sources = (k_ref, v_ref, q_ref)

    def piece(item, h, step):
        other, device = peer(step)
        return remote(
            sources[item].at[other * heads + h],
            landing(item, h, chip),
            send.at[h, item, step],
            recv.at[h, item, step],
            device,
        )

    def arriving(item, h, step):
        sender = lax.rem(chip + chips - step, chips)
        return remote(
            sources[item].at[h],
            landing(item, h, sender),
            send.at[h, item, step],
            recv.at[h, item, step],
            peer(step)[1],
        )

    def own_piece(item, h):
        return pltpu.make_async_copy(
            sources[item].at[chip * heads + h], landing(item, h, chip), own.at[h, item]
        )

    def list_piece(step):
        other, device = peer(step)
        return remote(
            lists_ref.at[other], lists_in.at[chip], list_send.at[step], list_recv.at[step], device
        )

    def list_arriving(step):
        sender = lax.rem(chip + chips - step, chips)
        return remote(
            lists_ref.at[0], lists_in.at[sender], list_send.at[step], list_recv.at[step], peer(step)[1]
        )

    list_own_copy = pltpu.make_async_copy(lists_ref.at[chip], lists_in.at[chip], list_own.at[0])
    steps = list(range(1, chips))
    for step in steps:
        list_piece(step).start()
    list_own_copy.start()
    for h in range(heads):
        for item in range(3):
            own_piece(item, h).start()
            for step in steps:
                piece(item, h, step).start()
    for step in steps:
        list_arriving(step).wait_recv()
    list_own_copy.wait()
    tokens = 2 * chips * rows
    lanes = lists_in.shape[-1]
    spread = (
        lax.broadcasted_iota(jnp.int32, (lanes, tokens), 1) // BLOCK
        == lax.broadcasted_iota(jnp.int32, (lanes, tokens), 0)
    ).astype(jnp.bfloat16)
    spread_lists = jnp.dot(
        lists_in[...].reshape(-1, lanes).astype(jnp.bfloat16),
        spread,
        preferred_element_type=jnp.float32,
    )
    members[...] = spread_lists.reshape(members.shape)

    def pair_piece(item, h):
        mine = pl.ds(core * half, half)
        buf = (k_bufs, v_bufs)[item][h]
        return remote(
            buf.at[mine], buf.at[mine], pair_send.at[h, item], pair_recv.at[h, item], mate
        )

    def pair_arriving(item, h):
        other = pl.ds((1 - core) * half, half)
        buf = (k_bufs, v_bufs)[item][h]
        return remote(
            buf.at[other], buf.at[other], pair_send.at[h, item], pair_recv.at[h, item], mate
        )

    def out_piece(h, step):
        other, device = peer(step)
        return remote(
            o_bufs[h].at[q_rows(other)],
            out_ref.at[chip * heads + h],
            out_send.at[h, step],
            out_recv.at[h, step],
            device,
        )

    def out_arriving(h, step):
        sender = lax.rem(chip + chips - step, chips)
        return remote(
            o_bufs[h].at[q_rows(sender)],
            out_ref.at[sender * heads + h],
            out_send.at[h, step],
            out_recv.at[h, step],
            peer(step)[1],
        )

    def out_own_piece(h):
        return pltpu.make_async_copy(
            o_bufs[h].at[q_rows(chip)], out_ref.at[chip * heads + h], out_own.at[h]
        )

    exponent_scale = math.log2(math.e) / math.sqrt(width)
    for h in range(heads):
        for item in range(2):
            own_piece(item, h).wait()
            for step in steps:
                arriving(item, h, step).wait_recv()
            pair_piece(item, h).start()
        own_piece(2, h).wait()
        for step in steps:
            arriving(2, h, step).wait_recv()
        for item in range(2):
            pair_arriving(item, h).wait_recv()

        k_buf, v_buf, q_buf, o_buf = k_bufs[h], v_bufs[h], q_bufs[h], o_bufs[h]
        for j in range(2 * chips):
            span = pl.ds(j * blocks, blocks)
            features[span] = wide_feature(k_buf[span]).astype(jnp.bfloat16)

        def one_shard(place, carry):
            span = pl.ds(place * blocks, blocks)
            query = q_buf[span].reshape(rows, width)
            narrow = wide_feature(query).astype(jnp.bfloat16)
            keys = k_buf[...].reshape(-1, width)
            key_features = features[...].reshape(-1, width)
            values = v_buf[...].reshape(-1, width)
            summed = jnp.concatenate([values, jnp.ones_like(values)], axis=1)
            scores = lax.dot_general(
                query, keys, (((1,), (1,)), ((), ())), preferred_element_type=jnp.float32
            )
            far = lax.dot_general(
                narrow, key_features, (((1,), (1,)), ((), ())), preferred_element_type=jnp.float32
            )
            expo, rest = [], []
            for b in range(blocks):
                listed_here = members[place, h, b : b + 1, :]
                part = scores[b * BLOCK : (b + 1) * BLOCK] + (listed_here - 1.0) * 1e30
                top = jnp.max(part, axis=-1, keepdims=True)
                expo.append(jnp.exp2((part - top) * exponent_scale).astype(jnp.bfloat16))
                part = far[b * BLOCK : (b + 1) * BLOCK] * (1.0 - listed_here)
                rest.append(part.astype(jnp.bfloat16))
            near_sums = jnp.dot(
                jnp.concatenate(expo, axis=0), summed, preferred_element_type=jnp.float32
            )
            far_sums = jnp.dot(
                jnp.concatenate(rest, axis=0), summed, preferred_element_type=jnp.float32
            )
            linear = (far_sums[:, :width] / far_sums[:, width:]).astype(jnp.bfloat16)
            projected = jnp.dot(linear, weight_ref[...], preferred_element_type=jnp.float32)
            mixed = near_sums[:, :width] / near_sums[:, width:] + projected
            o_buf[span] = mixed.astype(jnp.bfloat16).reshape(blocks, BLOCK, width)
            return carry

        lax.fori_loop(0, chips, one_shard, 0)
        for step in steps:
            out_piece(h, step).start()
        out_own_piece(h).start()

    for h in range(heads):
        for item in range(3):
            for step in steps:
                piece(item, h, step).wait_send()
        for item in range(2):
            pair_piece(item, h).wait_send()
        out_own_piece(h).wait()
        for step in steps:
            out_piece(h, step).wait_send()
            out_arriving(h, step).wait_recv()
    for step in steps:
        list_piece(step).wait_send()


def head_major(array):
    rows, heads, width = array.shape
    return array.transpose(1, 0, 2).reshape(heads, rows // BLOCK, BLOCK, width)


def by_heads(queries, key_rows, value_rows, critical, branch_weight):
    rows, all_heads, width = queries.shape
    blocks = rows // BLOCK
    chips = lax.axis_size("ctx")
    heads = all_heads // chips
    shard = critical // blocks
    place = (shard % 2) * (chips * blocks) + (shard // 2) * blocks + critical % blocks
    all_blocks = 2 * chips * blocks
    lanes = jnp.arange(all_blocks + -all_blocks % 128, dtype=jnp.int32)
    lists = jnp.any(place[..., None] == lanes, axis=2).astype(jnp.float32).transpose(1, 0, 2)
    lists = jnp.pad(lists, ((0, 0), (0, -blocks % 8), (0, 0)))
    lists = lists.reshape(chips, heads, blocks + -blocks % 8, lanes.shape[0])
    dims = (chips, heads, rows, width)
    hbm = pl.BlockSpec(memory_space=pl.ANY)
    vmem = pl.BlockSpec(memory_space=pltpu.VMEM)
    near = pltpu.VMEM((2 * chips * blocks, BLOCK, width), jnp.bfloat16)
    mine = pltpu.VMEM((chips * blocks, BLOCK, width), jnp.bfloat16)
    sem = pltpu.SemaphoreType.DMA
    pairs = heads * chips * blocks
    out = pl.pallas_call(
        functools.partial(by_heads_kernel, dims),
        out_shape=jax.ShapeDtypeStruct((all_heads, blocks, BLOCK, width), jnp.bfloat16),
        in_specs=[hbm, hbm, hbm, hbm, vmem],
        out_specs=hbm,
        scratch_shapes=[mine] * heads
        + [near] * heads
        + [near] * heads
        + [mine] * heads
        + [
            pltpu.VMEM(lists.shape, jnp.float32),
            pltpu.VMEM(lists.shape[:3] + (2 * chips * rows,), jnp.float32),
            near,
            sem((heads, 3, chips)),
            sem((heads, 3, chips)),
            sem((heads, 3)),
            sem((heads, 2)),
            sem((heads, 2)),
            sem((heads, chips)),
            sem((heads, chips)),
            sem((heads,)),
            sem((chips,)),
            sem((chips,)),
            sem((1,)),
        ],
        compiler_params=pltpu.CompilerParams(
            collective_id=0, has_side_effects=True, vmem_limit_bytes=56 * 1024 * 1024
        ),
        cost_estimate=pl.CostEstimate(
            flops=pairs * 8 * BLOCK * BLOCK * all_blocks * width,
            bytes_accessed=8 * all_heads * rows * width,
            transcendentals=pairs * BLOCK * BLOCK * all_blocks,
        ),
    )(
        head_major(queries),
        head_major(key_rows),
        head_major(value_rows),
        lists,
        branch_weight,
    )
    return out.reshape(all_heads, rows, width).transpose(1, 0, 2)


def heads_fit(mesh, queries, critical):
    chips, cores = mesh.shape["ctx"], mesh.shape["sub"]
    shards = mesh.shape["groups"] * chips * cores
    rows = queries.shape[0] // shards
    heads = queries.shape[1] // mesh.shape["head"]
    if cores != 2 or heads % chips or chips < 2 or rows % BLOCK:
        return False
    width = queries.shape[2]
    tokens = chips * cores * rows
    held = heads // chips * tokens * width * 2 * 3
    members = heads // chips * tokens * 4 * 8 * chips
    scores = rows * tokens * 4 * 4
    return held + members + scores < 32 * 1024 * 1024


def solution(mesh):
    in_specs = (
        P(("groups", "ctx", "sub"), "head", None),
        P(("groups", "ctx", "sub"), "head", None),
        P(("groups", "ctx", "sub"), "head", None),
        P(("groups", "ctx", "sub"), "head", None),
        P(),
    )
    out_specs = P(("groups", "ctx", "sub"), "head", None)

    def run(queries, key_rows, value_rows, critical, branch_weight):
        body = by_heads if heads_fit(mesh, queries, critical) else on_device
        mapped = jax.shard_map(
            body, mesh=mesh, in_specs=in_specs, out_specs=out_specs, check_vma=False
        )
        return mapped(queries, key_rows, value_rows, critical, branch_weight)

    return run
```

```python
import functools
import math

import jax
import jax.numpy as jnp
from jax import lax
from jax.experimental import pallas as pl
from jax.experimental.pallas import tpu as pltpu
from jax.sharding import PartitionSpec as P


def as_sent(array):

    def short(part):
        return part.astype(jnp.bfloat16) if part.dtype == jnp.float32 else part

    return jax.tree.map(short, array)


def feature(values_in):
    return jax.nn.elu(values_in) + 1.0


def attend_pair(inputs, pool_keys, pool_values, branch_weight, softmax_scale):
    query_block_rows, query_feature, pool_index, pair_state, pair_total = inputs
    block_count = query_block_rows.shape[0]
    head_width = query_block_rows.shape[-1]
    nearby_key_rows = jnp.take(pool_keys, pool_index.reshape(-1), axis=0).reshape(
        block_count, 2, -1, head_width
    )
    nearby_value_rows = jnp.take(pool_values, pool_index.reshape(-1), axis=0).reshape(
        block_count, 2, -1, head_width
    )
    score_matrix = (
        jnp.einsum(
            "bhqd,bhkd->bhqk", query_block_rows, nearby_key_rows, preferred_element_type=jnp.float32
        )
        * softmax_scale
    )
    top_score = jnp.max(score_matrix, axis=-1, keepdims=True)
    expo_scores = jnp.exp(score_matrix - top_score)
    softmax_weights = (expo_scores / jnp.sum(expo_scores, axis=-1, keepdims=True)).astype(
        jnp.bfloat16
    )
    sparse_output = jnp.einsum(
        "bhqk,bhkd->bhqd", softmax_weights, nearby_value_rows, preferred_element_type=jnp.float32
    )
    nearby_key_features = feature(nearby_key_rows.astype(jnp.float32)).astype(jnp.bfloat16)
    nearby_score_matrix = jnp.einsum(
        "bhqd,bhkd->bhqk", query_feature, nearby_key_features, preferred_element_type=jnp.float32
    )
    nearby_weight_matrix = nearby_score_matrix.astype(jnp.bfloat16)
    nearby_numerator = jnp.einsum(
        "bhqk,bhkd->bhqd",
        nearby_weight_matrix,
        nearby_value_rows,
        preferred_element_type=jnp.float32,
    )
    nearby_denominator = jnp.sum(nearby_score_matrix, axis=-1)
    feature_wide = query_feature.astype(jnp.float32)
    linear_numerator = (
        jnp.einsum("bhqd,hde->bhqe", feature_wide, pair_state, precision=lax.Precision.HIGHEST)
        - nearby_numerator
    )
    linear_denominator = (
        jnp.einsum("bhqd,hd->bhq", feature_wide, pair_total, precision=lax.Precision.HIGHEST)
        - nearby_denominator
    )
    linear_part = (linear_numerator / linear_denominator[..., None]).astype(jnp.bfloat16)
    projected = jnp.einsum(
        "bhqd,de->bhqe", linear_part, branch_weight, preferred_element_type=jnp.float32
    )
    return (sparse_output + projected).astype(jnp.bfloat16)


def on_device(queries, key_rows, value_rows, critical, branch_weight):
    row_count, head_count, head_width = queries.shape
    list_length = critical.shape[-1]
    block_count = row_count // 64
    shard_count = lax.axis_size(("ctx", "sub"))
    myself = lax.axis_index(("ctx", "sub"))
    local_count = min(block_count, 8)
    pool_size = 24 - local_count
    capacity = (head_count * pool_size + shard_count - 2) // (shard_count - 1)
    softmax_scale = head_width ** (-0.5)
    key_feature = feature(key_rows.astype(jnp.float32)).astype(jnp.bfloat16)
    query_feature = feature(queries.astype(jnp.float32)).astype(jnp.bfloat16)
    kv_state = jnp.einsum(
        "thd,the->hde", key_feature, value_rows, preferred_element_type=jnp.float32
    )
    key_total = jnp.sum(key_feature, axis=0, dtype=jnp.float32)
    kv_state, key_total = lax.psum((kv_state, key_total), ("ctx", "sub"))
    pair_slots = block_count * head_count
    block_owner = critical // block_count
    block_local = critical % block_count
    slot_code = block_local * head_count + jnp.arange(head_count, dtype=jnp.int32)[None, :, None]
    every_block = jnp.arange(shard_count * block_count, dtype=jnp.int32)
    hit_counts = jnp.sum((critical[..., None] == every_block).astype(jnp.int32), axis=(0, 2))
    wanted = (
        hit_counts.reshape(head_count, shard_count, block_count)
        .transpose(1, 2, 0)
        .reshape(shard_count, pair_slots)
        > 0
    )
    wanted = jnp.logical_and(wanted, jnp.arange(shard_count, dtype=jnp.int32)[:, None] != myself)
    slot_place = jnp.cumsum(wanted.astype(jnp.int32), axis=1) - 1
    slot_match = jnp.logical_and(
        wanted[:, :, None],
        slot_place[:, :, None] == jnp.arange(capacity, dtype=jnp.int32)[None, None, :],
    )
    code_values = jnp.sum(
        jnp.where(slot_match, jnp.arange(pair_slots, dtype=jnp.int32)[None, :, None], 0), axis=1
    )
    asked_codes = jnp.where(jnp.any(slot_match, axis=1), code_values, -1)
    local_keys = (
        key_rows.reshape(block_count, 64, head_count, head_width)
        .transpose(0, 2, 1, 3)
        .reshape(pair_slots, 64, head_width)
    )
    local_values = (
        value_rows.reshape(block_count, 64, head_count, head_width)
        .transpose(0, 2, 1, 3)
        .reshape(pair_slots, 64, head_width)
    )
    picked = jnp.clip(
        lax.all_to_all(asked_codes, ("ctx", "sub"), split_axis=0, concat_axis=0, tiled=True),
        0,
        pair_slots - 1,
    )
    far_keys, far_values = lax.all_to_all(
        as_sent((jnp.take(local_keys, picked, axis=0), jnp.take(local_values, picked, axis=0))),
        ("ctx", "sub"),
        split_axis=0,
        concat_axis=0,
        tiled=True,
    )
    pool_keys = jnp.concatenate(
        [local_keys, far_keys.reshape(shard_count * capacity, 64, head_width)], axis=0
    )
    pool_values = jnp.concatenate(
        [local_values, far_values.reshape(shard_count * capacity, 64, head_width)], axis=0
    )
    flat_index = block_owner * pair_slots + slot_code
    slot_table = jnp.where(wanted, slot_place, 0).reshape(-1)
    table_range = jnp.arange(shard_count * pair_slots, dtype=jnp.int32)
    slot_found = jnp.sum(jnp.where(flat_index[..., None] == table_range, slot_table, 0), axis=-1)
    pool_index = jnp.where(
        block_owner == myself, slot_code, pair_slots + block_owner * capacity + slot_found
    )
    pair_count = head_count // 2
    query_pairs = queries.reshape(block_count, 64, pair_count, 2, head_width).transpose(
        2, 0, 3, 1, 4
    )
    feature_pairs = query_feature.reshape(block_count, 64, pair_count, 2, head_width).transpose(
        2, 0, 3, 1, 4
    )
    index_pairs = pool_index.reshape(block_count, pair_count, 2, list_length).transpose(1, 0, 2, 3)
    state_pairs = kv_state.reshape(pair_count, 2, head_width, head_width)
    total_pairs = key_total.reshape(pair_count, 2, head_width)
    attended = lax.map(
        lambda inputs: attend_pair(inputs, pool_keys, pool_values, branch_weight, softmax_scale),
        (query_pairs, feature_pairs, index_pairs, state_pairs, total_pairs),
    )
    return attended.transpose(1, 3, 0, 2, 4).reshape(row_count, head_count, head_width)


BLOCK = 64


def wide_feature(rows):
    wide = rows.astype(jnp.float32)
    return jnp.where(wide > 0, wide + 1.0, jnp.exp(jnp.minimum(wide, 0.0)))


def by_heads_kernel(dims, *refs):
    chips, heads, rows, width = dims
    q_ref, k_ref, v_ref, lists_ref, weight_ref, out_ref = refs[:6]
    refs = refs[6:]
    q_bufs, refs = refs[:heads], refs[heads:]
    k_bufs, refs = refs[:heads], refs[heads:]
    v_bufs, refs = refs[:heads], refs[heads:]
    o_bufs, refs = refs[:heads], refs[heads:]
    lists_in, members, features, relay, out_relay = refs[:5]
    relay_send, relay_recv, pass_send, pass_recv = refs[5:9]
    out_relay_send, out_relay_recv, out_pass_send, out_pass_recv = refs[9:13]
    refs = refs[10:]
    (send, recv, own, pair_send, pair_recv, out_send, out_recv, out_own) = refs[3:11]
    list_send, list_recv, list_own = refs[11:]
    group = lax.axis_index("groups")
    chip = lax.axis_index("ctx")
    column = lax.axis_index("head")
    core = lax.axis_index("sub")
    blocks = rows // BLOCK
    half = chips * blocks
    piece_blocks = blocks // 2
    across = lax.rem(chip + 2, chips)
    mate = (group, chip, column, 1 - core)

    def peer(step):
        other = lax.rem(chip + step, chips)
        return other, (group, other, column, core)

    barrier = pltpu.get_barrier_semaphore()
    for step in range(1, chips):
        pl.semaphore_signal(barrier, inc=1, device_id=peer(step)[1], device_id_type=pl.DeviceIdType.MESH)
    pl.semaphore_signal(barrier, inc=1, device_id=mate, device_id_type=pl.DeviceIdType.MESH)
    pl.semaphore_wait(barrier, chips)

    def remote(src, dst, send_sem, recv_sem, device):
        return pltpu.make_async_remote_copy(
            src_ref=src,
            dst_ref=dst,
            send_sem=send_sem,
            recv_sem=recv_sem,
            device_id=device,
            device_id_type=pl.DeviceIdType.MESH,
        )

    def near_rows(place):
        return pl.ds(core * half + place * blocks, blocks)

    def q_rows(place):
        return pl.ds(place * blocks, blocks)

    def landing(item, h, place):
        if item == 2:
            return q_bufs[h].at[q_rows(place)]
        return (k_bufs, v_bufs)[item][h].at[near_rows(place)]

    sources = (k_ref, v_ref, q_ref)

    def piece(item, h, step):
        other, device = peer(step)
        return remote(
            sources[item].at[other * heads + h],
            landing(item, h, chip),
            send.at[h, item, step],
            recv.at[h, item, step],
            device,
        )

    def arriving(item, h, step):
        sender = lax.rem(chip + chips - step, chips)
        return remote(
            sources[item].at[h],
            landing(item, h, sender),
            send.at[h, item, step],
            recv.at[h, item, step],
            peer(step)[1],
        )

    def own_piece(item, h):
        return pltpu.make_async_copy(
            sources[item].at[chip * heads + h], landing(item, h, chip), own.at[h, item]
        )

    def list_piece(step):
        other, device = peer(step)
        return remote(
            lists_ref.at[other], lists_in.at[chip], list_send.at[step], list_recv.at[step], device
        )

    def list_arriving(step):
        sender = lax.rem(chip + chips - step, chips)
        return remote(
            lists_ref.at[0], lists_in.at[sender], list_send.at[step], list_recv.at[step], peer(step)[1]
        )

    ways = (1, chips - 1)

    def behind(way):
        return lax.rem(chip + chips - ways[way], chips)

    def part(way):
        return pl.ds(way * piece_blocks, piece_blocks)

    def landing_part(item, h, place, way):
        if item == 2:
            return q_bufs[h].at[pl.ds(place * blocks + way * piece_blocks, piece_blocks)]
        first = core * half + place * blocks + way * piece_blocks
        return (k_bufs, v_bufs)[item][h].at[pl.ds(first, piece_blocks)]

    def relay_piece(item, h, way):
        return remote(
            sources[item].at[across * heads + h, part(way)],
            relay.at[(h * 3 + item) * 2 + way],
            relay_send.at[h, item, way],
            relay_recv.at[h, item, way],
            peer(ways[way])[1],
        )

    def pass_piece(item, h, way):
        return remote(
            relay.at[(h * 3 + item) * 2 + way],
            landing_part(item, h, behind(way), way),
            pass_send.at[h, item, way],
            pass_recv.at[h, item, way],
            peer(ways[way])[1],
        )

    def pass_arriving(item, h, way):
        return remote(
            relay.at[(h * 3 + item) * 2 + way],
            landing_part(item, h, across, way),
            pass_send.at[h, item, way],
            pass_recv.at[h, item, way],
            peer(ways[way])[1],
        )

    def out_relay_piece(h, way):
        return remote(
            o_bufs[h].at[pl.ds(across * blocks + way * piece_blocks, piece_blocks)],
            out_relay.at[h * 2 + way],
            out_relay_send.at[h, way],
            out_relay_recv.at[h, way],
            peer(ways[way])[1],
        )

    def out_pass_piece(h, way):
        return remote(
            out_relay.at[h * 2 + way],
            out_ref.at[behind(way) * heads + h, part(way)],
            out_pass_send.at[h, way],
            out_pass_recv.at[h, way],
            peer(ways[way])[1],
        )

    def out_pass_arriving(h, way):
        return remote(
            out_relay.at[h * 2 + way],
            out_ref.at[across * heads + h, part(way)],
            out_pass_send.at[h, way],
            out_pass_recv.at[h, way],
            peer(ways[way])[1],
        )

    def send_head(h):
        for item in range(3):
            for way in range(2):
                relay_piece(item, h, way).start()
        for item in range(3):
            own_piece(item, h).start()
            for step in ways:
                piece(item, h, step).start()

    def pass_head(h):
        for item in range(3):
            for way in range(2):
                relay_piece(item, h, way).wait_recv()
                pass_piece(item, h, way).start()

    def pass_out(h):
        for way in range(2):
            out_relay_piece(h, way).wait_recv()
            out_pass_piece(h, way).start()

    list_own_copy = pltpu.make_async_copy(lists_ref.at[chip], lists_in.at[chip], list_own.at[0])
    steps = list(range(1, chips))
    for step in steps:
        list_piece(step).start()
    list_own_copy.start()
    for h in range(min(2, heads)):
        send_head(h)
    for step in steps:
        list_arriving(step).wait_recv()
    list_own_copy.wait()
    tokens = 2 * chips * rows
    lanes = lists_in.shape[-1]
    spread = (
        lax.broadcasted_iota(jnp.int32, (lanes, tokens), 1) // BLOCK
        == lax.broadcasted_iota(jnp.int32, (lanes, tokens), 0)
    ).astype(jnp.bfloat16)
    spread_lists = jnp.dot(
        lists_in[...].reshape(-1, lanes).astype(jnp.bfloat16),
        spread,
        preferred_element_type=jnp.float32,
    )
    members[...] = spread_lists.reshape(members.shape)

    def pair_piece(item, h):
        mine = pl.ds(core * half, half)
        buf = (k_bufs, v_bufs)[item][h]
        return remote(
            buf.at[mine], buf.at[mine], pair_send.at[h, item], pair_recv.at[h, item], mate
        )

    def pair_arriving(item, h):
        other = pl.ds((1 - core) * half, half)
        buf = (k_bufs, v_bufs)[item][h]
        return remote(
            buf.at[other], buf.at[other], pair_send.at[h, item], pair_recv.at[h, item], mate
        )

    def out_piece(h, step):
        other, device = peer(step)
        return remote(
            o_bufs[h].at[q_rows(other)],
            out_ref.at[chip * heads + h],
            out_send.at[h, step],
            out_recv.at[h, step],
            device,
        )

    def out_arriving(h, step):
        sender = lax.rem(chip + chips - step, chips)
        return remote(
            o_bufs[h].at[q_rows(sender)],
            out_ref.at[sender * heads + h],
            out_send.at[h, step],
            out_recv.at[h, step],
            peer(step)[1],
        )

    def out_own_piece(h):
        return pltpu.make_async_copy(
            o_bufs[h].at[q_rows(chip)], out_ref.at[chip * heads + h], out_own.at[h]
        )

    exponent_scale = math.log2(math.e) / math.sqrt(width)
    for h in range(heads):
        if h + 2 < heads:
            send_head(h + 2)
        if h == 0:
            pass_head(0)
        if h + 1 < heads:
            pass_head(h + 1)
        for item in range(2):
            own_piece(item, h).wait()
            for way in range(2):
                arriving(item, h, ways[way]).wait_recv()
                pass_arriving(item, h, way).wait_recv()
            pair_piece(item, h).start()
        own_piece(2, h).wait()
        for way in range(2):
            arriving(2, h, ways[way]).wait_recv()
            pass_arriving(2, h, way).wait_recv()
        for item in range(2):
            pair_arriving(item, h).wait_recv()

        k_buf, v_buf, q_buf, o_buf = k_bufs[h], v_bufs[h], q_bufs[h], o_bufs[h]
        for j in range(2 * chips):
            span = pl.ds(j * blocks, blocks)
            features[span] = wide_feature(k_buf[span]).astype(jnp.bfloat16)

        def one_shard(place, carry):
            span = pl.ds(place * blocks, blocks)
            query = q_buf[span].reshape(rows, width)
            narrow = wide_feature(query).astype(jnp.bfloat16)
            keys = k_buf[...].reshape(-1, width)
            key_features = features[...].reshape(-1, width)
            values = v_buf[...].reshape(-1, width)
            summed = jnp.concatenate([values, jnp.ones_like(values)], axis=1)
            scores = lax.dot_general(
                query, keys, (((1,), (1,)), ((), ())), preferred_element_type=jnp.float32
            )
            far = lax.dot_general(
                narrow, key_features, (((1,), (1,)), ((), ())), preferred_element_type=jnp.float32
            )
            expo, rest = [], []
            for b in range(blocks):
                listed_here = members[place, h, b : b + 1, :]
                part = scores[b * BLOCK : (b + 1) * BLOCK] + (listed_here - 1.0) * 1e30
                top = jnp.max(part, axis=-1, keepdims=True)
                expo.append(jnp.exp2((part - top) * exponent_scale).astype(jnp.bfloat16))
                part = far[b * BLOCK : (b + 1) * BLOCK] * (1.0 - listed_here)
                rest.append(part.astype(jnp.bfloat16))
            near_sums = jnp.dot(
                jnp.concatenate(expo, axis=0), summed, preferred_element_type=jnp.float32
            )
            far_sums = jnp.dot(
                jnp.concatenate(rest, axis=0), summed, preferred_element_type=jnp.float32
            )
            linear = (far_sums[:, :width] / far_sums[:, width:]).astype(jnp.bfloat16)
            projected = jnp.dot(linear, weight_ref[...], preferred_element_type=jnp.float32)
            mixed = near_sums[:, :width] / near_sums[:, width:] + projected
            o_buf[span] = mixed.astype(jnp.bfloat16).reshape(blocks, BLOCK, width)
            return carry

        lax.fori_loop(0, chips, one_shard, 0)
        for way in range(2):
            out_relay_piece(h, way).start()
        for step in ways:
            out_piece(h, step).start()
        out_own_piece(h).start()
        if h:
            pass_out(h - 1)
    pass_out(heads - 1)

    for h in range(heads):
        for way in range(2):
            for item in range(3):
                piece(item, h, ways[way]).wait_send()
                relay_piece(item, h, way).wait_send()
                pass_piece(item, h, way).wait_send()
            out_piece(h, ways[way]).wait_send()
            out_arriving(h, ways[way]).wait_recv()
            out_relay_piece(h, way).wait_send()
            out_pass_piece(h, way).wait_send()
            out_pass_arriving(h, way).wait_recv()
        for item in range(2):
            pair_piece(item, h).wait_send()
        out_own_piece(h).wait()
    for step in steps:
        list_piece(step).wait_send()


def head_major(array):
    rows, heads, width = array.shape
    return array.transpose(1, 0, 2).reshape(heads, rows // BLOCK, BLOCK, width)


def by_heads(queries, key_rows, value_rows, critical, branch_weight):
    rows, all_heads, width = queries.shape
    blocks = rows // BLOCK
    chips = lax.axis_size("ctx")
    heads = all_heads // chips
    shard = critical // blocks
    place = (shard % 2) * (chips * blocks) + (shard // 2) * blocks + critical % blocks
    all_blocks = 2 * chips * blocks
    lanes = jnp.arange(all_blocks + -all_blocks % 128, dtype=jnp.int32)
    lists = jnp.any(place[..., None] == lanes, axis=2).astype(jnp.float32).transpose(1, 0, 2)
    lists = jnp.pad(lists, ((0, 0), (0, -blocks % 8), (0, 0)))
    lists = lists.reshape(chips, heads, blocks + -blocks % 8, lanes.shape[0])
    dims = (chips, heads, rows, width)
    hbm = pl.BlockSpec(memory_space=pl.ANY)
    vmem = pl.BlockSpec(memory_space=pltpu.VMEM)
    near = pltpu.VMEM((2 * chips * blocks, BLOCK, width), jnp.bfloat16)
    mine = pltpu.VMEM((chips * blocks, BLOCK, width), jnp.bfloat16)
    sem = pltpu.SemaphoreType.DMA
    pairs = heads * chips * blocks
    out = pl.pallas_call(
        functools.partial(by_heads_kernel, dims),
        out_shape=jax.ShapeDtypeStruct((all_heads, blocks, BLOCK, width), jnp.bfloat16),
        in_specs=[hbm, hbm, hbm, hbm, vmem],
        out_specs=hbm,
        scratch_shapes=[mine] * heads
        + [near] * heads
        + [near] * heads
        + [mine] * heads
        + [
            pltpu.VMEM(lists.shape, jnp.float32),
            pltpu.VMEM(lists.shape[:3] + (2 * chips * rows,), jnp.float32),
            near,
            pltpu.VMEM((heads * 6, blocks // 2, BLOCK, width), jnp.bfloat16),
            pltpu.VMEM((heads * 2, blocks // 2, BLOCK, width), jnp.bfloat16),
            sem((heads, 3, 2)),
            sem((heads, 3, 2)),
            sem((heads, 3, 2)),
            sem((heads, 3, 2)),
            sem((heads, 2)),
            sem((heads, 2)),
            sem((heads, 2)),
            sem((heads, 2)),
            sem((heads, 3, chips)),
            sem((heads, 3, chips)),
            sem((heads, 3)),
            sem((heads, 2)),
            sem((heads, 2)),
            sem((heads, chips)),
            sem((heads, chips)),
            sem((heads,)),
            sem((chips,)),
            sem((chips,)),
            sem((1,)),
        ],
        compiler_params=pltpu.CompilerParams(
            collective_id=0, has_side_effects=True, vmem_limit_bytes=56 * 1024 * 1024
        ),
        cost_estimate=pl.CostEstimate(
            flops=pairs * 8 * BLOCK * BLOCK * all_blocks * width,
            bytes_accessed=8 * all_heads * rows * width,
            transcendentals=pairs * BLOCK * BLOCK * all_blocks,
        ),
    )(
        head_major(queries),
        head_major(key_rows),
        head_major(value_rows),
        lists,
        branch_weight,
    )
    return out.reshape(all_heads, rows, width).transpose(1, 0, 2)


def heads_fit(mesh, queries, critical):
    chips, cores = mesh.shape["ctx"], mesh.shape["sub"]
    shards = mesh.shape["groups"] * chips * cores
    rows = queries.shape[0] // shards
    heads = queries.shape[1] // mesh.shape["head"]
    if cores != 2 or heads % chips or chips != 4 or rows % (2 * BLOCK):
        return False
    width = queries.shape[2]
    tokens = chips * cores * rows
    held = heads // chips * tokens * width * 2 * 3
    members = heads // chips * tokens * 4 * 8 * chips
    scores = rows * tokens * 4 * 4
    return held + members + scores < 32 * 1024 * 1024


def solution(mesh):
    in_specs = (
        P(("groups", "ctx", "sub"), "head", None),
        P(("groups", "ctx", "sub"), "head", None),
        P(("groups", "ctx", "sub"), "head", None),
        P(("groups", "ctx", "sub"), "head", None),
        P(),
    )
    out_specs = P(("groups", "ctx", "sub"), "head", None)

    def run(queries, key_rows, value_rows, critical, branch_weight):
        body = by_heads if heads_fit(mesh, queries, critical) else on_device
        mapped = jax.shard_map(
            body, mesh=mesh, in_specs=in_specs, out_specs=out_specs, check_vma=False
        )
        return mapped(queries, key_rows, value_rows, critical, branch_weight)

    return run
```

```python
import functools
import math

import jax
import jax.numpy as jnp
from jax import lax
from jax.experimental import pallas as pl
from jax.experimental.pallas import tpu as pltpu
from jax.sharding import PartitionSpec as P


def as_sent(array):

    def short(part):
        return part.astype(jnp.bfloat16) if part.dtype == jnp.float32 else part

    return jax.tree.map(short, array)


def feature(values_in):
    return jax.nn.elu(values_in) + 1.0


def attend_pair(inputs, pool_keys, pool_values, branch_weight, softmax_scale):
    query_block_rows, query_feature, pool_index, pair_state, pair_total = inputs
    block_count = query_block_rows.shape[0]
    head_width = query_block_rows.shape[-1]
    nearby_key_rows = jnp.take(pool_keys, pool_index.reshape(-1), axis=0).reshape(
        block_count, 2, -1, head_width
    )
    nearby_value_rows = jnp.take(pool_values, pool_index.reshape(-1), axis=0).reshape(
        block_count, 2, -1, head_width
    )
    score_matrix = (
        jnp.einsum(
            "bhqd,bhkd->bhqk", query_block_rows, nearby_key_rows, preferred_element_type=jnp.float32
        )
        * softmax_scale
    )
    top_score = jnp.max(score_matrix, axis=-1, keepdims=True)
    expo_scores = jnp.exp(score_matrix - top_score)
    softmax_weights = (expo_scores / jnp.sum(expo_scores, axis=-1, keepdims=True)).astype(
        jnp.bfloat16
    )
    sparse_output = jnp.einsum(
        "bhqk,bhkd->bhqd", softmax_weights, nearby_value_rows, preferred_element_type=jnp.float32
    )
    nearby_key_features = feature(nearby_key_rows.astype(jnp.float32)).astype(jnp.bfloat16)
    nearby_score_matrix = jnp.einsum(
        "bhqd,bhkd->bhqk", query_feature, nearby_key_features, preferred_element_type=jnp.float32
    )
    nearby_weight_matrix = nearby_score_matrix.astype(jnp.bfloat16)
    nearby_numerator = jnp.einsum(
        "bhqk,bhkd->bhqd",
        nearby_weight_matrix,
        nearby_value_rows,
        preferred_element_type=jnp.float32,
    )
    nearby_denominator = jnp.sum(nearby_score_matrix, axis=-1)
    feature_wide = query_feature.astype(jnp.float32)
    linear_numerator = (
        jnp.einsum("bhqd,hde->bhqe", feature_wide, pair_state, precision=lax.Precision.HIGHEST)
        - nearby_numerator
    )
    linear_denominator = (
        jnp.einsum("bhqd,hd->bhq", feature_wide, pair_total, precision=lax.Precision.HIGHEST)
        - nearby_denominator
    )
    linear_part = (linear_numerator / linear_denominator[..., None]).astype(jnp.bfloat16)
    projected = jnp.einsum(
        "bhqd,de->bhqe", linear_part, branch_weight, preferred_element_type=jnp.float32
    )
    return (sparse_output + projected).astype(jnp.bfloat16)


def on_device(queries, key_rows, value_rows, critical, branch_weight):
    row_count, head_count, head_width = queries.shape
    list_length = critical.shape[-1]
    block_count = row_count // 64
    shard_count = lax.axis_size(("ctx", "sub"))
    myself = lax.axis_index(("ctx", "sub"))
    local_count = min(block_count, 8)
    pool_size = 24 - local_count
    capacity = (head_count * pool_size + shard_count - 2) // (shard_count - 1)
    softmax_scale = head_width ** (-0.5)
    key_feature = feature(key_rows.astype(jnp.float32)).astype(jnp.bfloat16)
    query_feature = feature(queries.astype(jnp.float32)).astype(jnp.bfloat16)
    kv_state = jnp.einsum(
        "thd,the->hde", key_feature, value_rows, preferred_element_type=jnp.float32
    )
    key_total = jnp.sum(key_feature, axis=0, dtype=jnp.float32)
    kv_state, key_total = lax.psum((kv_state, key_total), ("ctx", "sub"))
    pair_slots = block_count * head_count
    block_owner = critical // block_count
    block_local = critical % block_count
    slot_code = block_local * head_count + jnp.arange(head_count, dtype=jnp.int32)[None, :, None]
    every_block = jnp.arange(shard_count * block_count, dtype=jnp.int32)
    hit_counts = jnp.sum((critical[..., None] == every_block).astype(jnp.int32), axis=(0, 2))
    wanted = (
        hit_counts.reshape(head_count, shard_count, block_count)
        .transpose(1, 2, 0)
        .reshape(shard_count, pair_slots)
        > 0
    )
    wanted = jnp.logical_and(wanted, jnp.arange(shard_count, dtype=jnp.int32)[:, None] != myself)
    slot_place = jnp.cumsum(wanted.astype(jnp.int32), axis=1) - 1
    slot_match = jnp.logical_and(
        wanted[:, :, None],
        slot_place[:, :, None] == jnp.arange(capacity, dtype=jnp.int32)[None, None, :],
    )
    code_values = jnp.sum(
        jnp.where(slot_match, jnp.arange(pair_slots, dtype=jnp.int32)[None, :, None], 0), axis=1
    )
    asked_codes = jnp.where(jnp.any(slot_match, axis=1), code_values, -1)
    local_keys = (
        key_rows.reshape(block_count, 64, head_count, head_width)
        .transpose(0, 2, 1, 3)
        .reshape(pair_slots, 64, head_width)
    )
    local_values = (
        value_rows.reshape(block_count, 64, head_count, head_width)
        .transpose(0, 2, 1, 3)
        .reshape(pair_slots, 64, head_width)
    )
    picked = jnp.clip(
        lax.all_to_all(asked_codes, ("ctx", "sub"), split_axis=0, concat_axis=0, tiled=True),
        0,
        pair_slots - 1,
    )
    far_keys, far_values = lax.all_to_all(
        as_sent((jnp.take(local_keys, picked, axis=0), jnp.take(local_values, picked, axis=0))),
        ("ctx", "sub"),
        split_axis=0,
        concat_axis=0,
        tiled=True,
    )
    pool_keys = jnp.concatenate(
        [local_keys, far_keys.reshape(shard_count * capacity, 64, head_width)], axis=0
    )
    pool_values = jnp.concatenate(
        [local_values, far_values.reshape(shard_count * capacity, 64, head_width)], axis=0
    )
    flat_index = block_owner * pair_slots + slot_code
    slot_table = jnp.where(wanted, slot_place, 0).reshape(-1)
    table_range = jnp.arange(shard_count * pair_slots, dtype=jnp.int32)
    slot_found = jnp.sum(jnp.where(flat_index[..., None] == table_range, slot_table, 0), axis=-1)
    pool_index = jnp.where(
        block_owner == myself, slot_code, pair_slots + block_owner * capacity + slot_found
    )
    pair_count = head_count // 2
    query_pairs = queries.reshape(block_count, 64, pair_count, 2, head_width).transpose(
        2, 0, 3, 1, 4
    )
    feature_pairs = query_feature.reshape(block_count, 64, pair_count, 2, head_width).transpose(
        2, 0, 3, 1, 4
    )
    index_pairs = pool_index.reshape(block_count, pair_count, 2, list_length).transpose(1, 0, 2, 3)
    state_pairs = kv_state.reshape(pair_count, 2, head_width, head_width)
    total_pairs = key_total.reshape(pair_count, 2, head_width)
    attended = lax.map(
        lambda inputs: attend_pair(inputs, pool_keys, pool_values, branch_weight, softmax_scale),
        (query_pairs, feature_pairs, index_pairs, state_pairs, total_pairs),
    )
    return attended.transpose(1, 3, 0, 2, 4).reshape(row_count, head_count, head_width)


BLOCK = 64


def wide_feature(rows):
    wide = rows.astype(jnp.float32)
    return jnp.where(wide > 0, wide + 1.0, jnp.exp(jnp.minimum(wide, 0.0)))


def by_heads_kernel(dims, *refs):
    chips, heads, rows, width, listed = dims
    q_ref, k_ref, v_ref, lists_ref, weight_ref, out_ref = refs[:6]
    refs = refs[6:]
    q_bufs, refs = refs[:heads], refs[heads:]
    k_bufs, refs = refs[:heads], refs[heads:]
    v_bufs, refs = refs[:heads], refs[heads:]
    o_bufs, refs = refs[:heads], refs[heads:]
    (lists_in, lists, states, totals, scores, sparses, linears) = refs[:7]
    (send, recv, own, pair_send, pair_recv, out_send, out_recv, out_own) = refs[7:15]
    list_send, list_recv, list_own = refs[15:]
    group = lax.axis_index("groups")
    chip = lax.axis_index("ctx")
    column = lax.axis_index("head")
    core = lax.axis_index("sub")
    blocks = rows // BLOCK
    half = chips * blocks
    mate = (group, chip, column, 1 - core)

    def peer(step):
        other = lax.rem(chip + step, chips)
        return other, (group, other, column, core)

    barrier = pltpu.get_barrier_semaphore()
    for step in range(1, chips):
        pl.semaphore_signal(barrier, inc=1, device_id=peer(step)[1], device_id_type=pl.DeviceIdType.MESH)
    pl.semaphore_signal(barrier, inc=1, device_id=mate, device_id_type=pl.DeviceIdType.MESH)
    pl.semaphore_wait(barrier, chips)

    def remote(src, dst, send_sem, recv_sem, device):
        return pltpu.make_async_remote_copy(
            src_ref=src,
            dst_ref=dst,
            send_sem=send_sem,
            recv_sem=recv_sem,
            device_id=device,
            device_id_type=pl.DeviceIdType.MESH,
        )

    def near_rows(place):
        return pl.ds(core * half + place * blocks, blocks)

    def q_rows(place):
        return pl.ds(place * blocks, blocks)

    def landing(item, h, place):
        if item == 2:
            return q_bufs[h].at[q_rows(place)]
        return (k_bufs, v_bufs)[item][h].at[near_rows(place)]

    sources = (k_ref, v_ref, q_ref)

    def piece(item, h, step):
        other, device = peer(step)
        return remote(
            sources[item].at[other * heads + h],
            landing(item, h, chip),
            send.at[h, item, step],
            recv.at[h, item, step],
            device,
        )

    def arriving(item, h, step):
        sender = lax.rem(chip + chips - step, chips)
        return remote(
            sources[item].at[h],
            landing(item, h, sender),
            send.at[h, item, step],
            recv.at[h, item, step],
            peer(step)[1],
        )

    def own_piece(item, h):
        return pltpu.make_async_copy(
            sources[item].at[chip * heads + h], landing(item, h, chip), own.at[h, item]
        )

    def list_piece(step):
        other, device = peer(step)
        return remote(
            lists_ref.at[other], lists_in.at[chip], list_send.at[step], list_recv.at[step], device
        )

    def list_arriving(step):
        sender = lax.rem(chip + chips - step, chips)
        return remote(
            lists_ref.at[0], lists_in.at[sender], list_send.at[step], list_recv.at[step], peer(step)[1]
        )

    list_own_copy = pltpu.make_async_copy(lists_ref.at[chip], lists_in.at[chip], list_own.at[0])
    steps = list(range(1, chips))
    for step in steps:
        list_piece(step).start()
    list_own_copy.start()
    for h in range(heads):
        for item in range(3):
            own_piece(item, h).start()
            for step in steps:
                piece(item, h, step).start()
    for step in steps:
        list_arriving(step).wait_recv()
    list_own_copy.wait()
    to_scalars = pltpu.make_async_copy(lists_in, lists, list_own.at[1])
    to_scalars.start()
    to_scalars.wait()

    def pair_piece(item, h):
        mine = pl.ds(core * half, half)
        buf = (k_bufs, v_bufs)[item][h]
        return remote(
            buf.at[mine], buf.at[mine], pair_send.at[h, item], pair_recv.at[h, item], mate
        )

    def pair_arriving(item, h):
        other = pl.ds((1 - core) * half, half)
        buf = (k_bufs, v_bufs)[item][h]
        return remote(
            buf.at[other], buf.at[other], pair_send.at[h, item], pair_recv.at[h, item], mate
        )

    def out_piece(h, step):
        other, device = peer(step)
        return remote(
            o_bufs[h].at[q_rows(other)],
            out_ref.at[chip * heads + h],
            out_send.at[h, step],
            out_recv.at[h, step],
            device,
        )

    def out_arriving(h, step):
        sender = lax.rem(chip + chips - step, chips)
        return remote(
            o_bufs[h].at[q_rows(sender)],
            out_ref.at[sender * heads + h],
            out_send.at[h, step],
            out_recv.at[h, step],
            peer(step)[1],
        )

    def out_own_piece(h):
        return pltpu.make_async_copy(
            o_bufs[h].at[q_rows(chip)], out_ref.at[chip * heads + h], out_own.at[h]
        )

    exponent_scale = math.log2(math.e) / math.sqrt(width)

    def swap(h):
        for item in range(2):
            own_piece(item, h).wait()
            for step in steps:
                arriving(item, h, step).wait_recv()
            pair_piece(item, h).start()

    swap(0)
    for h in range(heads):
        own_piece(2, h).wait()
        for step in steps:
            arriving(2, h, step).wait_recv()
        for item in range(2):
            pair_arriving(item, h).wait_recv()

        k_buf, v_buf, q_buf, o_buf = k_bufs[h], v_bufs[h], q_bufs[h], o_bufs[h]

        def picks(b, first, count):
            place = b // blocks
            base = first * blocks + lax.rem(b, blocks) * count
            return [lists[place, h, base + i] for i in range(count)]

        def one_state(j, carry):
            narrow = wide_feature(k_buf[j]).astype(jnp.bfloat16)
            states[j] = lax.dot_general(
                narrow, v_buf[j], (((0,), (0,)), ((), ())), preferred_element_type=jnp.float32
            )
            totals[j] = jnp.sum(narrow.astype(jnp.float32).reshape(BLOCK // 8, 8, width), axis=0)
            return carry

        def one_score(b, carry):
            near_keys = jnp.concatenate([k_buf[pick] for pick in picks(b, 0, listed)], axis=0)
            scores[b] = lax.dot_general(
                q_buf[b], near_keys, (((1,), (1,)), ((), ())), preferred_element_type=jnp.float32
            )
            return carry

        def one_linear(b, carry):
            chosen = picks(b, listed, 2 * chips * blocks - listed)
            state = states[chosen[0]]
            total = totals[chosen[0]]
            for pick in chosen[1:]:
                state = state + states[pick]
                total = total + totals[pick]
            total = jnp.sum(total, axis=0, keepdims=True)
            coarse = state.astype(jnp.bfloat16)
            fine = (state - coarse.astype(jnp.float32)).astype(jnp.bfloat16)
            narrow = wide_feature(q_buf[b]).astype(jnp.bfloat16)
            numerator = jnp.dot(
                jnp.concatenate([narrow, narrow], axis=1),
                jnp.concatenate([coarse, fine], axis=0),
                preferred_element_type=jnp.float32,
            )
            denominator = jnp.sum(narrow.astype(jnp.float32) * total, axis=-1, keepdims=True)
            linears[b] = (numerator / denominator).astype(jnp.bfloat16)
            return carry

        def one_sparse(b, carry):
            near_values = jnp.concatenate([v_buf[pick] for pick in picks(b, 0, listed)], axis=0)
            here = scores[b]
            top = jnp.max(here, axis=-1, keepdims=True)
            expo = jnp.exp2((here - top) * exponent_scale)
            mass = jnp.sum(expo, axis=-1, keepdims=True)
            sparse = jnp.dot(
                expo.astype(jnp.bfloat16), near_values, preferred_element_type=jnp.float32
            )
            sparses[b] = sparse / mass
            return carry

        lax.fori_loop(0, chips * blocks, one_score, 0, unroll=4)
        lax.fori_loop(0, 2 * chips * blocks, one_state, 0, unroll=8)
        if h + 1 < heads:
            swap(h + 1)
        lax.fori_loop(0, chips * blocks, one_sparse, 0, unroll=4)
        lax.fori_loop(0, chips * blocks, one_linear, 0, unroll=4)
        projected = jnp.dot(
            linears[...].reshape(-1, width), weight_ref[...], preferred_element_type=jnp.float32
        )
        o_buf[...] = (sparses[...] + projected.reshape(sparses.shape)).astype(jnp.bfloat16)
        for step in steps:
            out_piece(h, step).start()
        out_own_piece(h).start()

    for h in range(heads):
        for item in range(3):
            for step in steps:
                piece(item, h, step).wait_send()
        for item in range(2):
            pair_piece(item, h).wait_send()
        out_own_piece(h).wait()
        for step in steps:
            out_piece(h, step).wait_send()
            out_arriving(h, step).wait_recv()
    for step in steps:
        list_piece(step).wait_send()


def head_major(array):
    rows, heads, width = array.shape
    return array.transpose(1, 0, 2).reshape(heads, rows // BLOCK, BLOCK, width)


def by_heads(queries, key_rows, value_rows, critical, branch_weight):
    rows, all_heads, width = queries.shape
    listed = critical.shape[-1]
    blocks = rows // BLOCK
    chips = lax.axis_size("ctx")
    heads = all_heads // chips
    shard = critical // blocks
    place = (shard % 2) * (chips * blocks) + (shard // 2) * blocks + critical % blocks
    all_blocks = 2 * chips * blocks
    every = jnp.arange(all_blocks, dtype=jnp.int32)
    unlisted = jnp.all(place[..., None] != every, axis=2)
    earlier = jnp.logical_and(unlisted[..., None, :], every[None, :] < every[:, None])
    rank = jnp.where(unlisted, jnp.sum(earlier.astype(jnp.int32), axis=-1), -1)
    ranks = jnp.arange(all_blocks - listed, dtype=jnp.int32)
    others = jnp.sum(jnp.where(rank[..., None, :] == ranks[:, None], every, 0), axis=-1)
    lists = jnp.concatenate(
        [
            rows_of.transpose(1, 0, 2).reshape(chips, heads, -1)
            for rows_of in (place, others)
        ],
        axis=-1,
    )
    lists = jnp.pad(lists, ((0, 0), (0, -heads % 8), (0, -lists.shape[-1] % 128)))
    dims = (chips, heads, rows, width, listed)
    hbm = pl.BlockSpec(memory_space=pl.ANY)
    vmem = pl.BlockSpec(memory_space=pltpu.VMEM)
    near = pltpu.VMEM((2 * chips * blocks, BLOCK, width), jnp.bfloat16)
    mine = pltpu.VMEM((chips * blocks, BLOCK, width), jnp.bfloat16)
    sem = pltpu.SemaphoreType.DMA
    pairs = heads * chips * blocks
    out = pl.pallas_call(
        functools.partial(by_heads_kernel, dims),
        out_shape=jax.ShapeDtypeStruct((all_heads, blocks, BLOCK, width), jnp.bfloat16),
        in_specs=[hbm, hbm, hbm, hbm, vmem],
        out_specs=hbm,
        scratch_shapes=[mine] * heads
        + [near] * heads
        + [near] * heads
        + [mine] * heads
        + [
            pltpu.VMEM(lists.shape, jnp.int32),
            pltpu.SMEM(lists.shape, jnp.int32),
            pltpu.VMEM((all_blocks, width, width), jnp.float32),
            pltpu.VMEM((all_blocks, 8, width), jnp.float32),
            pltpu.VMEM((chips * blocks, BLOCK, listed * BLOCK), jnp.float32),
            pltpu.VMEM((chips * blocks, BLOCK, width), jnp.float32),
            mine,
            sem((heads, 3, chips)),
            sem((heads, 3, chips)),
            sem((heads, 3)),
            sem((heads, 2)),
            sem((heads, 2)),
            sem((heads, chips)),
            sem((heads, chips)),
            sem((heads,)),
            sem((chips,)),
            sem((chips,)),
            sem((2,)),
        ],
        compiler_params=pltpu.CompilerParams(
            collective_id=0, has_side_effects=True, vmem_limit_bytes=56 * 1024 * 1024
        ),
        cost_estimate=pl.CostEstimate(
            flops=pairs * 4 * BLOCK * BLOCK * listed * width,
            bytes_accessed=8 * all_heads * rows * width,
            transcendentals=pairs * BLOCK * BLOCK * listed,
        ),
    )(
        head_major(queries),
        head_major(key_rows),
        head_major(value_rows),
        lists,
        branch_weight,
    )
    return out.reshape(all_heads, rows, width).transpose(1, 0, 2)


def heads_fit(mesh, queries, critical):
    chips, cores = mesh.shape["ctx"], mesh.shape["sub"]
    shards = mesh.shape["groups"] * chips * cores
    rows = queries.shape[0] // shards
    heads = queries.shape[1] // mesh.shape["head"]
    if cores != 2 or heads % chips or chips < 2 or rows % BLOCK:
        return False
    width = queries.shape[2]
    tokens = chips * cores * rows
    held = heads // chips * tokens * width * 2 * 3
    states = tokens // BLOCK * (width + 8) * width * 4
    scores = chips * rows * (critical.shape[2] * BLOCK + 2 * width) * 4
    if critical.shape[2] >= tokens // BLOCK:
        return False
    return held + states + scores < 40 * 1024 * 1024


def solution(mesh):
    in_specs = (
        P(("groups", "ctx", "sub"), "head", None),
        P(("groups", "ctx", "sub"), "head", None),
        P(("groups", "ctx", "sub"), "head", None),
        P(("groups", "ctx", "sub"), "head", None),
        P(),
    )
    out_specs = P(("groups", "ctx", "sub"), "head", None)

    def run(queries, key_rows, value_rows, critical, branch_weight):
        body = by_heads if heads_fit(mesh, queries, critical) else on_device
        mapped = jax.shard_map(
            body, mesh=mesh, in_specs=in_specs, out_specs=out_specs, check_vma=False
        )
        return mapped(queries, key_rows, value_rows, critical, branch_weight)

    return run
```

```python
import functools
import math

import jax
import jax.numpy as jnp
from jax import lax
from jax.experimental import pallas as pl
from jax.experimental.pallas import tpu as pltpu
from jax.sharding import PartitionSpec as P


def as_sent(array):

    def short(part):
        return part.astype(jnp.bfloat16) if part.dtype == jnp.float32 else part

    return jax.tree.map(short, array)


def feature(values_in):
    return jax.nn.elu(values_in) + 1.0


def attend_pair(inputs, pool_keys, pool_values, branch_weight, softmax_scale):
    query_block_rows, query_feature, pool_index, pair_state, pair_total = inputs
    block_count = query_block_rows.shape[0]
    head_width = query_block_rows.shape[-1]
    nearby_key_rows = jnp.take(pool_keys, pool_index.reshape(-1), axis=0).reshape(
        block_count, 2, -1, head_width
    )
    nearby_value_rows = jnp.take(pool_values, pool_index.reshape(-1), axis=0).reshape(
        block_count, 2, -1, head_width
    )
    score_matrix = (
        jnp.einsum(
            "bhqd,bhkd->bhqk", query_block_rows, nearby_key_rows, preferred_element_type=jnp.float32
        )
        * softmax_scale
    )
    top_score = jnp.max(score_matrix, axis=-1, keepdims=True)
    expo_scores = jnp.exp(score_matrix - top_score)
    softmax_weights = (expo_scores / jnp.sum(expo_scores, axis=-1, keepdims=True)).astype(
        jnp.bfloat16
    )
    sparse_output = jnp.einsum(
        "bhqk,bhkd->bhqd", softmax_weights, nearby_value_rows, preferred_element_type=jnp.float32
    )
    nearby_key_features = feature(nearby_key_rows.astype(jnp.float32)).astype(jnp.bfloat16)
    nearby_score_matrix = jnp.einsum(
        "bhqd,bhkd->bhqk", query_feature, nearby_key_features, preferred_element_type=jnp.float32
    )
    nearby_weight_matrix = nearby_score_matrix.astype(jnp.bfloat16)
    nearby_numerator = jnp.einsum(
        "bhqk,bhkd->bhqd",
        nearby_weight_matrix,
        nearby_value_rows,
        preferred_element_type=jnp.float32,
    )
    nearby_denominator = jnp.sum(nearby_score_matrix, axis=-1)
    feature_wide = query_feature.astype(jnp.float32)
    linear_numerator = (
        jnp.einsum("bhqd,hde->bhqe", feature_wide, pair_state, precision=lax.Precision.HIGHEST)
        - nearby_numerator
    )
    linear_denominator = (
        jnp.einsum("bhqd,hd->bhq", feature_wide, pair_total, precision=lax.Precision.HIGHEST)
        - nearby_denominator
    )
    linear_part = (linear_numerator / linear_denominator[..., None]).astype(jnp.bfloat16)
    projected = jnp.einsum(
        "bhqd,de->bhqe", linear_part, branch_weight, preferred_element_type=jnp.float32
    )
    return (sparse_output + projected).astype(jnp.bfloat16)


def on_device(queries, key_rows, value_rows, critical, branch_weight):
    row_count, head_count, head_width = queries.shape
    list_length = critical.shape[-1]
    block_count = row_count // 64
    shard_count = lax.axis_size(("ctx", "sub"))
    myself = lax.axis_index(("ctx", "sub"))
    local_count = min(block_count, 8)
    pool_size = 24 - local_count
    capacity = (head_count * pool_size + shard_count - 2) // (shard_count - 1)
    softmax_scale = head_width ** (-0.5)
    key_feature = feature(key_rows.astype(jnp.float32)).astype(jnp.bfloat16)
    query_feature = feature(queries.astype(jnp.float32)).astype(jnp.bfloat16)
    kv_state = jnp.einsum(
        "thd,the->hde", key_feature, value_rows, preferred_element_type=jnp.float32
    )
    key_total = jnp.sum(key_feature, axis=0, dtype=jnp.float32)
    kv_state, key_total = lax.psum((kv_state, key_total), ("ctx", "sub"))
    pair_slots = block_count * head_count
    block_owner = critical // block_count
    block_local = critical % block_count
    slot_code = block_local * head_count + jnp.arange(head_count, dtype=jnp.int32)[None, :, None]
    every_block = jnp.arange(shard_count * block_count, dtype=jnp.int32)
    hit_counts = jnp.sum((critical[..., None] == every_block).astype(jnp.int32), axis=(0, 2))
    wanted = (
        hit_counts.reshape(head_count, shard_count, block_count)
        .transpose(1, 2, 0)
        .reshape(shard_count, pair_slots)
        > 0
    )
    wanted = jnp.logical_and(wanted, jnp.arange(shard_count, dtype=jnp.int32)[:, None] != myself)
    slot_place = jnp.cumsum(wanted.astype(jnp.int32), axis=1) - 1
    slot_match = jnp.logical_and(
        wanted[:, :, None],
        slot_place[:, :, None] == jnp.arange(capacity, dtype=jnp.int32)[None, None, :],
    )
    code_values = jnp.sum(
        jnp.where(slot_match, jnp.arange(pair_slots, dtype=jnp.int32)[None, :, None], 0), axis=1
    )
    asked_codes = jnp.where(jnp.any(slot_match, axis=1), code_values, -1)
    local_keys = (
        key_rows.reshape(block_count, 64, head_count, head_width)
        .transpose(0, 2, 1, 3)
        .reshape(pair_slots, 64, head_width)
    )
    local_values = (
        value_rows.reshape(block_count, 64, head_count, head_width)
        .transpose(0, 2, 1, 3)
        .reshape(pair_slots, 64, head_width)
    )
    picked = jnp.clip(
        lax.all_to_all(asked_codes, ("ctx", "sub"), split_axis=0, concat_axis=0, tiled=True),
        0,
        pair_slots - 1,
    )
    far_keys, far_values = lax.all_to_all(
        as_sent((jnp.take(local_keys, picked, axis=0), jnp.take(local_values, picked, axis=0))),
        ("ctx", "sub"),
        split_axis=0,
        concat_axis=0,
        tiled=True,
    )
    pool_keys = jnp.concatenate(
        [local_keys, far_keys.reshape(shard_count * capacity, 64, head_width)], axis=0
    )
    pool_values = jnp.concatenate(
        [local_values, far_values.reshape(shard_count * capacity, 64, head_width)], axis=0
    )
    flat_index = block_owner * pair_slots + slot_code
    slot_table = jnp.where(wanted, slot_place, 0).reshape(-1)
    table_range = jnp.arange(shard_count * pair_slots, dtype=jnp.int32)
    slot_found = jnp.sum(jnp.where(flat_index[..., None] == table_range, slot_table, 0), axis=-1)
    pool_index = jnp.where(
        block_owner == myself, slot_code, pair_slots + block_owner * capacity + slot_found
    )
    pair_count = head_count // 2
    query_pairs = queries.reshape(block_count, 64, pair_count, 2, head_width).transpose(
        2, 0, 3, 1, 4
    )
    feature_pairs = query_feature.reshape(block_count, 64, pair_count, 2, head_width).transpose(
        2, 0, 3, 1, 4
    )
    index_pairs = pool_index.reshape(block_count, pair_count, 2, list_length).transpose(1, 0, 2, 3)
    state_pairs = kv_state.reshape(pair_count, 2, head_width, head_width)
    total_pairs = key_total.reshape(pair_count, 2, head_width)
    attended = lax.map(
        lambda inputs: attend_pair(inputs, pool_keys, pool_values, branch_weight, softmax_scale),
        (query_pairs, feature_pairs, index_pairs, state_pairs, total_pairs),
    )
    return attended.transpose(1, 3, 0, 2, 4).reshape(row_count, head_count, head_width)


BLOCK = 64


def wide_feature(rows):
    wide = rows.astype(jnp.float32)
    return jnp.where(wide > 0, wide + 1.0, jnp.exp(jnp.minimum(wide, 0.0)))


def by_heads_kernel(dims, *refs):
    chips, heads, rows, width = dims
    q_ref, k_ref, v_ref, lists_ref, weight_ref, out_ref = refs[:6]
    refs = refs[6:]
    q_bufs, refs = refs[:heads], refs[heads:]
    k_bufs, refs = refs[:heads], refs[heads:]
    v_bufs, refs = refs[:heads], refs[heads:]
    o_bufs, refs = refs[:heads], refs[heads:]
    lists_in, members, features = refs[:3]
    (send, recv, own, pair_send, pair_recv, out_send, out_recv, out_own) = refs[3:11]
    list_send, list_recv, list_own = refs[11:]
    group = lax.axis_index("groups")
    chip = lax.axis_index("ctx")
    column = lax.axis_index("head")
    core = lax.axis_index("sub")
    blocks = rows // BLOCK
    half = chips * blocks
    mate = (group, chip, column, 1 - core)

    def peer(step):
        other = lax.rem(chip + step, chips)
        return other, (group, other, column, core)

    barrier = pltpu.get_barrier_semaphore()
    for step in range(1, chips):
        pl.semaphore_signal(barrier, inc=1, device_id=peer(step)[1], device_id_type=pl.DeviceIdType.MESH)
    pl.semaphore_signal(barrier, inc=1, device_id=mate, device_id_type=pl.DeviceIdType.MESH)
    pl.semaphore_wait(barrier, chips)

    def remote(src, dst, send_sem, recv_sem, device):
        return pltpu.make_async_remote_copy(
            src_ref=src,
            dst_ref=dst,
            send_sem=send_sem,
            recv_sem=recv_sem,
            device_id=device,
            device_id_type=pl.DeviceIdType.MESH,
        )

    def near_rows(place):
        return pl.ds(core * half + place * blocks, blocks)

    def q_rows(place):
        return pl.ds(place * blocks, blocks)

    def landing(item, h, place):
        if item == 2:
            return q_bufs[h].at[q_rows(place)]
        return (k_bufs, v_bufs)[item][h].at[near_rows(place)]

    sources = (k_ref, v_ref, q_ref)

    def piece(item, h, step):
        other, device = peer(step)
        return remote(
            sources[item].at[other * heads + h],
            landing(item, h, chip),
            send.at[h, item, step],
            recv.at[h, item, step],
            device,
        )

    def arriving(item, h, step):
        sender = lax.rem(chip + chips - step, chips)
        return remote(
            sources[item].at[h],
            landing(item, h, sender),
            send.at[h, item, step],
            recv.at[h, item, step],
            peer(step)[1],
        )

    def own_piece(item, h):
        return pltpu.make_async_copy(
            sources[item].at[chip * heads + h], landing(item, h, chip), own.at[h, item]
        )

    def list_piece(step):
        other, device = peer(step)
        return remote(
            lists_ref.at[other], lists_in.at[chip], list_send.at[step], list_recv.at[step], device
        )

    def list_arriving(step):
        sender = lax.rem(chip + chips - step, chips)
        return remote(
            lists_ref.at[0], lists_in.at[sender], list_send.at[step], list_recv.at[step], peer(step)[1]
        )

    list_own_copy = pltpu.make_async_copy(lists_ref.at[chip], lists_in.at[chip], list_own.at[0])
    steps = list(range(1, chips))
    for step in steps:
        list_piece(step).start()
    list_own_copy.start()

    def send_rows(item, h):
        for step in steps:
            piece(item, h, step).start()
        own_piece(item, h).start()

    for h in range(heads):
        send_rows(0, h)
        send_rows(1, h)
        if h:
            send_rows(2, h - 1)
    send_rows(2, heads - 1)
    for step in steps:
        list_arriving(step).wait_recv()
    list_own_copy.wait()
    tokens = 2 * chips * rows
    lanes = lists_in.shape[-1]
    spread = (
        lax.broadcasted_iota(jnp.int32, (lanes, tokens), 1) // BLOCK
        == lax.broadcasted_iota(jnp.int32, (lanes, tokens), 0)
    ).astype(jnp.bfloat16)
    spread_lists = jnp.dot(
        lists_in[...].reshape(-1, lanes).astype(jnp.bfloat16),
        spread,
        preferred_element_type=jnp.float32,
    )
    members[...] = spread_lists.reshape(members.shape)

    def pair_piece(item, h):
        mine = pl.ds(core * half, half)
        buf = (k_bufs, v_bufs)[item][h]
        return remote(
            buf.at[mine], buf.at[mine], pair_send.at[h, item], pair_recv.at[h, item], mate
        )

    def pair_arriving(item, h):
        other = pl.ds((1 - core) * half, half)
        buf = (k_bufs, v_bufs)[item][h]
        return remote(
            buf.at[other], buf.at[other], pair_send.at[h, item], pair_recv.at[h, item], mate
        )

    def out_piece(h, step):
        other, device = peer(step)
        return remote(
            o_bufs[h].at[q_rows(other)],
            out_ref.at[chip * heads + h],
            out_send.at[h, step],
            out_recv.at[h, step],
            device,
        )

    def out_arriving(h, step):
        sender = lax.rem(chip + chips - step, chips)
        return remote(
            o_bufs[h].at[q_rows(sender)],
            out_ref.at[sender * heads + h],
            out_send.at[h, step],
            out_recv.at[h, step],
            peer(step)[1],
        )

    def out_own_piece(h):
        return pltpu.make_async_copy(
            o_bufs[h].at[q_rows(chip)], out_ref.at[chip * heads + h], out_own.at[h]
        )

    exponent_scale = math.log2(math.e) / math.sqrt(width)

    def swap(h):
        for item in range(2):
            own_piece(item, h).wait()
            for step in steps:
                arriving(item, h, step).wait_recv()
            pair_piece(item, h).start()

    swap(0)
    for h in range(heads):
        if h + 1 < heads:
            swap(h + 1)
        for item in range(2):
            pair_arriving(item, h).wait_recv()

        k_buf, v_buf, q_buf, o_buf = k_bufs[h], v_bufs[h], q_bufs[h], o_bufs[h]
        for j in range(2 * chips):
            span = pl.ds(j * blocks, blocks)
            features[span] = wide_feature(k_buf[span]).astype(jnp.bfloat16)

        def one_shard(step, carry):
            place = lax.rem(chip + chips - step, chips)

            @pl.when(step == 0)
            def _():
                own_piece(2, h).wait()

            @pl.when(step > 0)
            def _():
                arriving(2, h, step).wait_recv()

            span = pl.ds(place * blocks, blocks)
            query = q_buf[span].reshape(rows, width)
            narrow = wide_feature(query).astype(jnp.bfloat16)
            keys = k_buf[...].reshape(-1, width)
            key_features = features[...].reshape(-1, width)
            values = v_buf[...].reshape(-1, width)
            summed = jnp.concatenate([values, jnp.ones_like(values)], axis=1)
            scores = lax.dot_general(
                query, keys, (((1,), (1,)), ((), ())), preferred_element_type=jnp.float32
            )
            far = lax.dot_general(
                narrow, key_features, (((1,), (1,)), ((), ())), preferred_element_type=jnp.float32
            )
            expo, rest = [], []
            for b in range(blocks):
                listed_here = members[place, h, b : b + 1, :]
                part = scores[b * BLOCK : (b + 1) * BLOCK] + (listed_here - 1.0) * 1e30
                top = jnp.max(part, axis=-1, keepdims=True)
                expo.append(jnp.exp2((part - top) * exponent_scale).astype(jnp.bfloat16))
                part = far[b * BLOCK : (b + 1) * BLOCK] * (1.0 - listed_here)
                rest.append(part.astype(jnp.bfloat16))
            near_sums = jnp.dot(
                jnp.concatenate(expo, axis=0), summed, preferred_element_type=jnp.float32
            )
            far_sums = jnp.dot(
                jnp.concatenate(rest, axis=0), summed, preferred_element_type=jnp.float32
            )
            linear = (far_sums[:, :width] / far_sums[:, width:]).astype(jnp.bfloat16)
            projected = jnp.dot(linear, weight_ref[...], preferred_element_type=jnp.float32)
            mixed = near_sums[:, :width] / near_sums[:, width:] + projected
            o_buf[span] = mixed.astype(jnp.bfloat16).reshape(blocks, BLOCK, width)

            @pl.when(step == 0)
            def _():
                out_own_piece(h).start()

            @pl.when(step > 0)
            def _():
                out_piece(h, chips - step).start()

            return carry

        lax.fori_loop(0, chips, one_shard, 0)

    for h in range(heads):
        for item in range(3):
            for step in steps:
                piece(item, h, step).wait_send()
        for item in range(2):
            pair_piece(item, h).wait_send()
        out_own_piece(h).wait()
        for step in steps:
            out_piece(h, step).wait_send()
            out_arriving(h, step).wait_recv()
    for step in steps:
        list_piece(step).wait_send()


def head_major(array):
    rows, heads, width = array.shape
    return array.transpose(1, 0, 2).reshape(heads, rows // BLOCK, BLOCK, width)


def by_heads(queries, key_rows, value_rows, critical, branch_weight):
    rows, all_heads, width = queries.shape
    blocks = rows // BLOCK
    chips = lax.axis_size("ctx")
    heads = all_heads // chips
    shard = critical // blocks
    place = (shard % 2) * (chips * blocks) + (shard // 2) * blocks + critical % blocks
    all_blocks = 2 * chips * blocks
    lanes = jnp.arange(all_blocks + -all_blocks % 128, dtype=jnp.int32)
    lists = jnp.any(place[..., None] == lanes, axis=2).astype(jnp.float32).transpose(1, 0, 2)
    lists = jnp.pad(lists, ((0, 0), (0, -blocks % 8), (0, 0)))
    lists = lists.reshape(chips, heads, blocks + -blocks % 8, lanes.shape[0])
    dims = (chips, heads, rows, width)
    hbm = pl.BlockSpec(memory_space=pl.ANY)
    vmem = pl.BlockSpec(memory_space=pltpu.VMEM)
    near = pltpu.VMEM((2 * chips * blocks, BLOCK, width), jnp.bfloat16)
    mine = pltpu.VMEM((chips * blocks, BLOCK, width), jnp.bfloat16)
    sem = pltpu.SemaphoreType.DMA
    pairs = heads * chips * blocks
    out = pl.pallas_call(
        functools.partial(by_heads_kernel, dims),
        out_shape=jax.ShapeDtypeStruct((all_heads, blocks, BLOCK, width), jnp.bfloat16),
        in_specs=[hbm, hbm, hbm, hbm, vmem],
        out_specs=hbm,
        scratch_shapes=[mine] * heads
        + [near] * heads
        + [near] * heads
        + [mine] * heads
        + [
            pltpu.VMEM(lists.shape, jnp.float32),
            pltpu.VMEM(lists.shape[:3] + (2 * chips * rows,), jnp.float32),
            near,
            sem((heads, 3, chips)),
            sem((heads, 3, chips)),
            sem((heads, 3)),
            sem((heads, 2)),
            sem((heads, 2)),
            sem((heads, chips)),
            sem((heads, chips)),
            sem((heads,)),
            sem((chips,)),
            sem((chips,)),
            sem((1,)),
        ],
        compiler_params=pltpu.CompilerParams(
            collective_id=0, has_side_effects=True, vmem_limit_bytes=56 * 1024 * 1024
        ),
        cost_estimate=pl.CostEstimate(
            flops=pairs * 8 * BLOCK * BLOCK * all_blocks * width,
            bytes_accessed=8 * all_heads * rows * width,
            transcendentals=pairs * BLOCK * BLOCK * all_blocks,
        ),
    )(
        head_major(queries),
        head_major(key_rows),
        head_major(value_rows),
        lists,
        branch_weight,
    )
    return out.reshape(all_heads, rows, width).transpose(1, 0, 2)


def heads_fit(mesh, queries, critical):
    chips, cores = mesh.shape["ctx"], mesh.shape["sub"]
    shards = mesh.shape["groups"] * chips * cores
    rows = queries.shape[0] // shards
    heads = queries.shape[1] // mesh.shape["head"]
    if cores != 2 or heads % chips or chips < 2 or rows % BLOCK:
        return False
    width = queries.shape[2]
    tokens = chips * cores * rows
    held = heads // chips * tokens * width * 2 * 3
    members = heads // chips * tokens * 4 * 8 * chips
    scores = rows * tokens * 4 * 4
    return held + members + scores < 32 * 1024 * 1024


def solution(mesh):
    in_specs = (
        P(("groups", "ctx", "sub"), "head", None),
        P(("groups", "ctx", "sub"), "head", None),
        P(("groups", "ctx", "sub"), "head", None),
        P(("groups", "ctx", "sub"), "head", None),
        P(),
    )
    out_specs = P(("groups", "ctx", "sub"), "head", None)

    def run(queries, key_rows, value_rows, critical, branch_weight):
        body = by_heads if heads_fit(mesh, queries, critical) else on_device
        mapped = jax.shard_map(
            body, mesh=mesh, in_specs=in_specs, out_specs=out_specs, check_vma=False
        )
        return mapped(queries, key_rows, value_rows, critical, branch_weight)

    return run
```

```python
import functools
import math

import jax
import jax.numpy as jnp
from jax import lax
from jax.experimental import pallas as pl
from jax.experimental.pallas import tpu as pltpu
from jax.sharding import PartitionSpec as P


def as_sent(array):

    def short(part):
        return part.astype(jnp.bfloat16) if part.dtype == jnp.float32 else part

    return jax.tree.map(short, array)


def feature(values_in):
    return jax.nn.elu(values_in) + 1.0


def attend_pair(inputs, pool_keys, pool_values, branch_weight, softmax_scale):
    query_block_rows, query_feature, pool_index, pair_state, pair_total = inputs
    block_count = query_block_rows.shape[0]
    head_width = query_block_rows.shape[-1]
    nearby_key_rows = jnp.take(pool_keys, pool_index.reshape(-1), axis=0).reshape(
        block_count, 2, -1, head_width
    )
    nearby_value_rows = jnp.take(pool_values, pool_index.reshape(-1), axis=0).reshape(
        block_count, 2, -1, head_width
    )
    score_matrix = (
        jnp.einsum(
            "bhqd,bhkd->bhqk", query_block_rows, nearby_key_rows, preferred_element_type=jnp.float32
        )
        * softmax_scale
    )
    top_score = jnp.max(score_matrix, axis=-1, keepdims=True)
    expo_scores = jnp.exp(score_matrix - top_score)
    softmax_weights = (expo_scores / jnp.sum(expo_scores, axis=-1, keepdims=True)).astype(
        jnp.bfloat16
    )
    sparse_output = jnp.einsum(
        "bhqk,bhkd->bhqd", softmax_weights, nearby_value_rows, preferred_element_type=jnp.float32
    )
    nearby_key_features = feature(nearby_key_rows.astype(jnp.float32)).astype(jnp.bfloat16)
    nearby_score_matrix = jnp.einsum(
        "bhqd,bhkd->bhqk", query_feature, nearby_key_features, preferred_element_type=jnp.float32
    )
    nearby_weight_matrix = nearby_score_matrix.astype(jnp.bfloat16)
    nearby_numerator = jnp.einsum(
        "bhqk,bhkd->bhqd",
        nearby_weight_matrix,
        nearby_value_rows,
        preferred_element_type=jnp.float32,
    )
    nearby_denominator = jnp.sum(nearby_score_matrix, axis=-1)
    feature_wide = query_feature.astype(jnp.float32)
    linear_numerator = (
        jnp.einsum("bhqd,hde->bhqe", feature_wide, pair_state, precision=lax.Precision.HIGHEST)
        - nearby_numerator
    )
    linear_denominator = (
        jnp.einsum("bhqd,hd->bhq", feature_wide, pair_total, precision=lax.Precision.HIGHEST)
        - nearby_denominator
    )
    linear_part = (linear_numerator / linear_denominator[..., None]).astype(jnp.bfloat16)
    projected = jnp.einsum(
        "bhqd,de->bhqe", linear_part, branch_weight, preferred_element_type=jnp.float32
    )
    return (sparse_output + projected).astype(jnp.bfloat16)


def on_device(queries, key_rows, value_rows, critical, branch_weight):
    row_count, head_count, head_width = queries.shape
    list_length = critical.shape[-1]
    block_count = row_count // 64
    shard_count = lax.axis_size(("ctx", "sub"))
    myself = lax.axis_index(("ctx", "sub"))
    local_count = min(block_count, 8)
    pool_size = 24 - local_count
    capacity = (head_count * pool_size + shard_count - 2) // (shard_count - 1)
    softmax_scale = head_width ** (-0.5)
    key_feature = feature(key_rows.astype(jnp.float32)).astype(jnp.bfloat16)
    query_feature = feature(queries.astype(jnp.float32)).astype(jnp.bfloat16)
    kv_state = jnp.einsum(
        "thd,the->hde", key_feature, value_rows, preferred_element_type=jnp.float32
    )
    key_total = jnp.sum(key_feature, axis=0, dtype=jnp.float32)
    kv_state, key_total = lax.psum((kv_state, key_total), ("ctx", "sub"))
    pair_slots = block_count * head_count
    block_owner = critical // block_count
    block_local = critical % block_count
    slot_code = block_local * head_count + jnp.arange(head_count, dtype=jnp.int32)[None, :, None]
    every_block = jnp.arange(shard_count * block_count, dtype=jnp.int32)
    hit_counts = jnp.sum((critical[..., None] == every_block).astype(jnp.int32), axis=(0, 2))
    wanted = (
        hit_counts.reshape(head_count, shard_count, block_count)
        .transpose(1, 2, 0)
        .reshape(shard_count, pair_slots)
        > 0
    )
    wanted = jnp.logical_and(wanted, jnp.arange(shard_count, dtype=jnp.int32)[:, None] != myself)
    slot_place = jnp.cumsum(wanted.astype(jnp.int32), axis=1) - 1
    slot_match = jnp.logical_and(
        wanted[:, :, None],
        slot_place[:, :, None] == jnp.arange(capacity, dtype=jnp.int32)[None, None, :],
    )
    code_values = jnp.sum(
        jnp.where(slot_match, jnp.arange(pair_slots, dtype=jnp.int32)[None, :, None], 0), axis=1
    )
    asked_codes = jnp.where(jnp.any(slot_match, axis=1), code_values, -1)
    local_keys = (
        key_rows.reshape(block_count, 64, head_count, head_width)
        .transpose(0, 2, 1, 3)
        .reshape(pair_slots, 64, head_width)
    )
    local_values = (
        value_rows.reshape(block_count, 64, head_count, head_width)
        .transpose(0, 2, 1, 3)
        .reshape(pair_slots, 64, head_width)
    )
    picked = jnp.clip(
        lax.all_to_all(asked_codes, ("ctx", "sub"), split_axis=0, concat_axis=0, tiled=True),
        0,
        pair_slots - 1,
    )
    far_keys, far_values = lax.all_to_all(
        as_sent((jnp.take(local_keys, picked, axis=0), jnp.take(local_values, picked, axis=0))),
        ("ctx", "sub"),
        split_axis=0,
        concat_axis=0,
        tiled=True,
    )
    pool_keys = jnp.concatenate(
        [local_keys, far_keys.reshape(shard_count * capacity, 64, head_width)], axis=0
    )
    pool_values = jnp.concatenate(
        [local_values, far_values.reshape(shard_count * capacity, 64, head_width)], axis=0
    )
    flat_index = block_owner * pair_slots + slot_code
    slot_table = jnp.where(wanted, slot_place, 0).reshape(-1)
    table_range = jnp.arange(shard_count * pair_slots, dtype=jnp.int32)
    slot_found = jnp.sum(jnp.where(flat_index[..., None] == table_range, slot_table, 0), axis=-1)
    pool_index = jnp.where(
        block_owner == myself, slot_code, pair_slots + block_owner * capacity + slot_found
    )
    pair_count = head_count // 2
    query_pairs = queries.reshape(block_count, 64, pair_count, 2, head_width).transpose(
        2, 0, 3, 1, 4
    )
    feature_pairs = query_feature.reshape(block_count, 64, pair_count, 2, head_width).transpose(
        2, 0, 3, 1, 4
    )
    index_pairs = pool_index.reshape(block_count, pair_count, 2, list_length).transpose(1, 0, 2, 3)
    state_pairs = kv_state.reshape(pair_count, 2, head_width, head_width)
    total_pairs = key_total.reshape(pair_count, 2, head_width)
    attended = lax.map(
        lambda inputs: attend_pair(inputs, pool_keys, pool_values, branch_weight, softmax_scale),
        (query_pairs, feature_pairs, index_pairs, state_pairs, total_pairs),
    )
    return attended.transpose(1, 3, 0, 2, 4).reshape(row_count, head_count, head_width)


BLOCK = 64


def wide_feature(rows):
    wide = rows.astype(jnp.float32)
    return jnp.where(wide > 0, wide + 1.0, jnp.exp(jnp.minimum(wide, 0.0)))


def by_heads_kernel(dims, *refs):
    chips, heads, rows, width = dims
    q_ref, k_ref, v_ref, lists_ref, weight_ref, out_ref = refs[:6]
    refs = refs[6:]
    q_bufs, refs = refs[:heads], refs[heads:]
    k_bufs, refs = refs[:heads], refs[heads:]
    v_bufs, refs = refs[:heads], refs[heads:]
    o_bufs, refs = refs[:heads], refs[heads:]
    lists_in, members, features = refs[:3]
    (send, recv, own, pair_send, pair_recv, out_send, out_recv, out_own) = refs[3:11]
    list_send, list_recv, list_own = refs[11:]
    group = lax.axis_index("groups")
    chip = lax.axis_index("ctx")
    column = lax.axis_index("head")
    core = lax.axis_index("sub")
    blocks = rows // BLOCK
    half = chips * blocks
    mate = (group, chip, column, 1 - core)

    def peer(step):
        other = lax.rem(chip + step, chips)
        return other, (group, other, column, core)

    barrier = pltpu.get_barrier_semaphore()
    for step in range(1, chips):
        pl.semaphore_signal(barrier, inc=1, device_id=peer(step)[1], device_id_type=pl.DeviceIdType.MESH)
    pl.semaphore_signal(barrier, inc=1, device_id=mate, device_id_type=pl.DeviceIdType.MESH)
    pl.semaphore_wait(barrier, chips)

    def remote(src, dst, send_sem, recv_sem, device):
        return pltpu.make_async_remote_copy(
            src_ref=src,
            dst_ref=dst,
            send_sem=send_sem,
            recv_sem=recv_sem,
            device_id=device,
            device_id_type=pl.DeviceIdType.MESH,
        )

    def near_rows(place):
        return pl.ds(core * half + place * blocks, blocks)

    def q_rows(place):
        return pl.ds(place * blocks, blocks)

    def landing(item, h, place):
        if item == 2:
            return q_bufs[h].at[q_rows(place)]
        return (k_bufs, v_bufs)[item][h].at[near_rows(place)]

    sources = (k_ref, v_ref, q_ref)

    def piece(item, h, step):
        other, device = peer(step)
        return remote(
            sources[item].at[other * heads + h],
            landing(item, h, chip),
            send.at[h, item, step],
            recv.at[h, item, step],
            device,
        )

    def arriving(item, h, step):
        sender = lax.rem(chip + chips - step, chips)
        return remote(
            sources[item].at[h],
            landing(item, h, sender),
            send.at[h, item, step],
            recv.at[h, item, step],
            peer(step)[1],
        )

    def own_piece(item, h):
        return pltpu.make_async_copy(
            sources[item].at[chip * heads + h], landing(item, h, chip), own.at[h, item]
        )

    def list_piece(step):
        other, device = peer(step)
        return remote(
            lists_ref.at[other], lists_in.at[chip], list_send.at[step], list_recv.at[step], device
        )

    def list_arriving(step):
        sender = lax.rem(chip + chips - step, chips)
        return remote(
            lists_ref.at[0], lists_in.at[sender], list_send.at[step], list_recv.at[step], peer(step)[1]
        )

    list_own_copy = pltpu.make_async_copy(lists_ref.at[chip], lists_in.at[chip], list_own.at[0])
    steps = list(range(1, chips))
    for step in steps:
        list_piece(step).start()
    list_own_copy.start()

    def send_rows(item, h):
        for step in steps:
            piece(item, h, step).start()
        own_piece(item, h).start()

    for h in range(min(2, heads)):
        send_rows(0, h)
        send_rows(1, h)
    send_rows(2, 0)
    for step in steps:
        list_arriving(step).wait_recv()
    list_own_copy.wait()
    tokens = 2 * chips * rows
    lanes = lists_in.shape[-1]
    spread = (
        lax.broadcasted_iota(jnp.int32, (lanes, tokens), 1) // BLOCK
        == lax.broadcasted_iota(jnp.int32, (lanes, tokens), 0)
    ).astype(jnp.bfloat16)
    spread_lists = jnp.dot(
        lists_in[...].reshape(-1, lanes).astype(jnp.bfloat16),
        spread,
        preferred_element_type=jnp.float32,
    )
    members[...] = spread_lists.reshape(members.shape)

    def pair_piece(item, h):
        mine = pl.ds(core * half, half)
        buf = (k_bufs, v_bufs)[item][h]
        return remote(
            buf.at[mine], buf.at[mine], pair_send.at[h, item], pair_recv.at[h, item], mate
        )

    def pair_arriving(item, h):
        other = pl.ds((1 - core) * half, half)
        buf = (k_bufs, v_bufs)[item][h]
        return remote(
            buf.at[other], buf.at[other], pair_send.at[h, item], pair_recv.at[h, item], mate
        )

    def out_piece(h, step):
        other, device = peer(step)
        return remote(
            o_bufs[h].at[q_rows(other)],
            out_ref.at[chip * heads + h],
            out_send.at[h, step],
            out_recv.at[h, step],
            device,
        )

    def out_arriving(h, step):
        sender = lax.rem(chip + chips - step, chips)
        return remote(
            o_bufs[h].at[q_rows(sender)],
            out_ref.at[sender * heads + h],
            out_send.at[h, step],
            out_recv.at[h, step],
            peer(step)[1],
        )

    def out_own_piece(h):
        return pltpu.make_async_copy(
            o_bufs[h].at[q_rows(chip)], out_ref.at[chip * heads + h], out_own.at[h]
        )

    exponent_scale = math.log2(math.e) / math.sqrt(width)

    def swap(h):
        for item in range(2):
            own_piece(item, h).wait()
            for step in steps:
                arriving(item, h, step).wait_recv()
            pair_piece(item, h).start()

    swap(0)
    for h in range(heads):
        if h + 2 < heads:
            send_rows(0, h + 2)
            send_rows(1, h + 2)
        if h + 1 < heads:
            send_rows(2, h + 1)
            swap(h + 1)
        for item in range(2):
            pair_arriving(item, h).wait_recv()

        k_buf, v_buf, q_buf, o_buf = k_bufs[h], v_bufs[h], q_bufs[h], o_bufs[h]
        for j in range(2 * chips):
            span = pl.ds(j * blocks, blocks)
            features[span] = wide_feature(k_buf[span]).astype(jnp.bfloat16)

        def one_shard(step, carry):
            place = lax.rem(chip + chips - step, chips)

            @pl.when(step == 0)
            def _():
                own_piece(2, h).wait()

            @pl.when(step > 0)
            def _():
                arriving(2, h, step).wait_recv()

            span = pl.ds(place * blocks, blocks)
            query = q_buf[span].reshape(rows, width)
            narrow = wide_feature(query).astype(jnp.bfloat16)
            keys = k_buf[...].reshape(-1, width)
            key_features = features[...].reshape(-1, width)
            values = v_buf[...].reshape(-1, width)
            summed = jnp.concatenate([values, jnp.ones_like(values)], axis=1)
            scores = lax.dot_general(
                query, keys, (((1,), (1,)), ((), ())), preferred_element_type=jnp.float32
            )
            far = lax.dot_general(
                narrow, key_features, (((1,), (1,)), ((), ())), preferred_element_type=jnp.float32
            )
            expo, rest = [], []
            for b in range(blocks):
                listed_here = members[place, h, b : b + 1, :]
                part = scores[b * BLOCK : (b + 1) * BLOCK] + (listed_here - 1.0) * 1e30
                top = jnp.max(part, axis=-1, keepdims=True)
                expo.append(jnp.exp2((part - top) * exponent_scale).astype(jnp.bfloat16))
                part = far[b * BLOCK : (b + 1) * BLOCK] * (1.0 - listed_here)
                rest.append(part.astype(jnp.bfloat16))
            near_sums = jnp.dot(
                jnp.concatenate(expo, axis=0), summed, preferred_element_type=jnp.float32
            )
            far_sums = jnp.dot(
                jnp.concatenate(rest, axis=0), summed, preferred_element_type=jnp.float32
            )
            linear = (far_sums[:, :width] / far_sums[:, width:]).astype(jnp.bfloat16)
            projected = jnp.dot(linear, weight_ref[...], preferred_element_type=jnp.float32)
            mixed = near_sums[:, :width] / near_sums[:, width:] + projected
            o_buf[span] = mixed.astype(jnp.bfloat16).reshape(blocks, BLOCK, width)

            @pl.when(step == 0)
            def _():
                out_own_piece(h).start()

            @pl.when(step > 0)
            def _():
                out_piece(h, chips - step).start()

            return carry

        lax.fori_loop(0, chips, one_shard, 0)

    for h in range(heads):
        for item in range(3):
            for step in steps:
                piece(item, h, step).wait_send()
        for item in range(2):
            pair_piece(item, h).wait_send()
        out_own_piece(h).wait()
        for step in steps:
            out_piece(h, step).wait_send()
            out_arriving(h, step).wait_recv()
    for step in steps:
        list_piece(step).wait_send()


def head_major(array):
    rows, heads, width = array.shape
    return array.transpose(1, 0, 2).reshape(heads, rows // BLOCK, BLOCK, width)


def by_heads(queries, key_rows, value_rows, critical, branch_weight):
    rows, all_heads, width = queries.shape
    blocks = rows // BLOCK
    chips = lax.axis_size("ctx")
    heads = all_heads // chips
    shard = critical // blocks
    place = (shard % 2) * (chips * blocks) + (shard // 2) * blocks + critical % blocks
    all_blocks = 2 * chips * blocks
    lanes = jnp.arange(all_blocks + -all_blocks % 128, dtype=jnp.int32)
    lists = jnp.any(place[..., None] == lanes, axis=2).astype(jnp.float32).transpose(1, 0, 2)
    lists = jnp.pad(lists, ((0, 0), (0, -blocks % 8), (0, 0)))
    lists = lists.reshape(chips, heads, blocks + -blocks % 8, lanes.shape[0])
    dims = (chips, heads, rows, width)
    hbm = pl.BlockSpec(memory_space=pl.ANY)
    vmem = pl.BlockSpec(memory_space=pltpu.VMEM)
    near = pltpu.VMEM((2 * chips * blocks, BLOCK, width), jnp.bfloat16)
    mine = pltpu.VMEM((chips * blocks, BLOCK, width), jnp.bfloat16)
    sem = pltpu.SemaphoreType.DMA
    pairs = heads * chips * blocks
    out = pl.pallas_call(
        functools.partial(by_heads_kernel, dims),
        out_shape=jax.ShapeDtypeStruct((all_heads, blocks, BLOCK, width), jnp.bfloat16),
        in_specs=[hbm, hbm, hbm, hbm, vmem],
        out_specs=hbm,
        scratch_shapes=[mine] * heads
        + [near] * heads
        + [near] * heads
        + [mine] * heads
        + [
            pltpu.VMEM(lists.shape, jnp.float32),
            pltpu.VMEM(lists.shape[:3] + (2 * chips * rows,), jnp.float32),
            near,
            sem((heads, 3, chips)),
            sem((heads, 3, chips)),
            sem((heads, 3)),
            sem((heads, 2)),
            sem((heads, 2)),
            sem((heads, chips)),
            sem((heads, chips)),
            sem((heads,)),
            sem((chips,)),
            sem((chips,)),
            sem((1,)),
        ],
        compiler_params=pltpu.CompilerParams(
            collective_id=0, has_side_effects=True, vmem_limit_bytes=56 * 1024 * 1024
        ),
        cost_estimate=pl.CostEstimate(
            flops=pairs * 8 * BLOCK * BLOCK * all_blocks * width,
            bytes_accessed=8 * all_heads * rows * width,
            transcendentals=pairs * BLOCK * BLOCK * all_blocks,
        ),
    )(
        head_major(queries),
        head_major(key_rows),
        head_major(value_rows),
        lists,
        branch_weight,
    )
    return out.reshape(all_heads, rows, width).transpose(1, 0, 2)


def heads_fit(mesh, queries, critical):
    chips, cores = mesh.shape["ctx"], mesh.shape["sub"]
    shards = mesh.shape["groups"] * chips * cores
    rows = queries.shape[0] // shards
    heads = queries.shape[1] // mesh.shape["head"]
    if cores != 2 or heads % chips or chips < 2 or rows % BLOCK:
        return False
    width = queries.shape[2]
    tokens = chips * cores * rows
    held = heads // chips * tokens * width * 2 * 3
    members = heads // chips * tokens * 4 * 8 * chips
    scores = rows * tokens * 4 * 4
    return held + members + scores < 32 * 1024 * 1024


def solution(mesh):
    in_specs = (
        P(("groups", "ctx", "sub"), "head", None),
        P(("groups", "ctx", "sub"), "head", None),
        P(("groups", "ctx", "sub"), "head", None),
        P(("groups", "ctx", "sub"), "head", None),
        P(),
    )
    out_specs = P(("groups", "ctx", "sub"), "head", None)

    def run(queries, key_rows, value_rows, critical, branch_weight):
        body = by_heads if heads_fit(mesh, queries, critical) else on_device
        mapped = jax.shard_map(
            body, mesh=mesh, in_specs=in_specs, out_specs=out_specs, check_vma=False
        )
        return mapped(queries, key_rows, value_rows, critical, branch_weight)

    return run
```
